256 devices in a mesh: heads: 4 (over x), ctx: 64 (over z, y, core).
Axes of the slice: x: 4, y: 4, z: 8, core: 2. Of those that a mesh axis runs over, the one named last changes fastest.
Arguments:
- context_q: bfloat16 [16384, 8192], P('ctx', 'heads'), may hold values from -120 to 120
- context_k: bfloat16 [16384, 1024], P('ctx', 'heads'), may hold values from -8 to 8, as said below
- context_v: bfloat16 [16384, 1024], P('ctx', 'heads'), may hold values from -6 to 6
- question: bfloat16 [256, 8192], P('ctx', 'heads'), may hold values from -120 to 120
- block_lengths: int32 [64], replicated, may hold values from 1 to 256, 12288 in all
- anchor_index: int32 [64], replicated, may hold values from 0 to 63, each once
- question_length: int32 [1], replicated, may hold values from 128 to 256
Outputs:
- mixed: bfloat16 [16384, 8192], P('ctx', 'heads')
- key_cache: bfloat16 [16384, 1024], P('ctx', 'heads')
- value_cache: bfloat16 [16384, 1024], P('ctx', 'heads')
- answer: bfloat16 [256, 8192], P(None, 'heads')
The draws below stay inside these ranges and needn't reach their ends.
Inputs may be any that keep to these rules, and one draw needn't show every extreme that they name: `context_k`: real values of order one. `block_lengths`: the lengths sum to three quarters of 16384; some block is full. `anchor_index`: each block number appears once.
All inputs are finite; a program needn't handle non-finite values.
Results may differ from the reference program's by a relative error of at most 0.0034.
The reference program's roundings to bfloat16 on the way count: a program that leaves them out, or rounds other values in their place, can miss the bound.
Values may be sent and summed in bfloat16 or wider, within the bound.
No kernel may reach another device: no remote copies, remote signals or barrier semaphores. Data moves between devices by JAX's collectives and lax.ppermute only.
A program may use at most 320 MiB of HBM per device.

```python
import math
import jax
import jax.numpy as jnp
import numpy as np
from jax import lax

QH = 64
KVH = 8
HD = 128
BLK = 256
QLEN = 256
NBLK = 64
TOKENS = 16384


def shared_keys(key):
    return jax.random.normal(key, (TOKENS, KVH * HD), jnp.float32)


def draw_context_k(key, part):
    base = shared_keys(key)
    return jnp.clip(base, -8.0, 8.0).astype(jnp.bfloat16)


def draw_context_q(key, part):
    key = jax.random.fold_in(key, 2)
    first_key = jax.random.fold_in(key, 0)
    values = jax.random.normal(first_key, (TOKENS, QH * HD), jnp.float32)
    return jnp.clip(values, -120.0, 120.0).astype(jnp.bfloat16)


def draw_question(key, part):
    key = jax.random.fold_in(key, 3)
    first_key = jax.random.fold_in(key, 0)
    values = jax.random.normal(first_key, (QLEN, QH * HD), jnp.float32)
    return jnp.clip(values, -120.0, 120.0).astype(jnp.bfloat16)


def shard_levels(key, shape, cuts, least, top_value):
    factor_of = 1.0
    for axis_at, parts in cuts:
        steps = jax.random.uniform(jax.random.fold_in(jax.random.fold_in(key, 6), axis_at), (parts,), jnp.float32, least / len(cuts), top_value / len(cuts))
        factor_of = factor_of * jnp.repeat(jnp.exp(steps), shape[axis_at] // parts).reshape((-1,) + (1,) * (len(shape) - 1 - axis_at))
    return factor_of


def length_profile(count, total, reach, lean):
    portions = [(1 << 20) // math.isqrt(standing ** lean) + 1 for standing in range(2, count + 1)]
    rest, counts = total - reach - (count - 1), [1] * (count - 1)
    while rest > 0:
        movable = [i for i in range(count - 1) if counts[i] < reach]
        mass, left = sum([portions[i] for i in movable]), rest
        for i in movable:
            extra = min(reach - counts[i], max(1, left * portions[i] // mass), rest)
            counts[i] = counts[i] + extra
            rest = rest - extra
    return np.array([reach] + counts)


def ragged(key, amount, total, most, skew):
    if amount == 2:
        one = jax.random.randint(key, (), max(1, total - most), min(most, total - 1) + 1)
        return jnp.stack([one, total - one])
    sizes = jnp.asarray(length_profile(amount, total, most, skew), jnp.int32)
    twos = (amount - 1) // 2
    source_of, receiver = sizes[1:1 + 2 * twos:2], sizes[2:2 + 2 * twos:2]
    room = jnp.minimum(source_of - 1, most - receiver)
    moved = jax.random.randint(jax.random.fold_in(key, 1), (twos,), 0, 1 << 20) % (room + 1)
    sizes = sizes.at[1:1 + 2 * twos:2].set(source_of - moved).at[2:2 + 2 * twos:2].set(receiver + moved)
    return sizes[jax.random.permutation(jax.random.fold_in(key, 2), amount)]


def gaussian(rng, extent, scale, most, shards=(), kind=jnp.bfloat16):
    drawn = jax.random.normal(rng, extent, jnp.float32) * scale
    if len(shards) > 0:
        drawn = shard_levels(rng, extent, shards, -0.22, 0.18) * drawn
    return jnp.clip(drawn, min=-most, max=most).astype(kind)


def setup_inputs(seed: int = 0) -> dict:
    seeds = jax.random.split(jax.random.key(seed), 8)
    return {
        "context_q": draw_context_q(jax.random.fold_in(seeds[7], 71), 0),
        "context_k": draw_context_k(jax.random.fold_in(seeds[7], 71), 0),
        "context_v": gaussian(seeds[2], (TOKENS, KVH * HD), 1.0, 6.0, ((0, 64), (1, 4))),
        "question": draw_question(jax.random.fold_in(seeds[7], 71), 0),
        "block_lengths": ragged(seeds[4], NBLK, NBLK * BLK * 3 // 4, BLK, 0).astype(jnp.int32),
        "anchor_index": jax.random.permutation(seeds[5], NBLK).astype(jnp.int32),
        "question_length": jax.random.randint(seeds[6], (1,), QLEN // 2, QLEN + 1).astype(jnp.int32),
    }


def sign_table(count):
    index = np.arange(count)
    both = index[:, None] & index[None, :]
    parity = np.zeros((count, count), np.int64)
    for bit_place in range(16):
        parity = parity ^ ((both >> bit_place) & 1)
    return jnp.asarray(1 - 2 * parity, jnp.bfloat16)


def rotate(rows, table):
    flat = rows.reshape(-1, HD)
    turned = jnp.dot(flat, table, preferred_element_type=jnp.float32) * (HD ** -0.5)
    return turned.astype(jnp.bfloat16).reshape(rows.shape)


def encode_block(q_b, k_b, v_b, anchor_k, anchor_v, length, anchor_len, is_anchor):
    factor = HD ** -0.5
    queries = q_b.astype(jnp.float32)
    s_far = jnp.einsum('tgjd,sgd->tgjs', queries, anchor_k.astype(jnp.float32)) * factor
    s_own = jnp.einsum('tgjd,sgd->tgjs', queries, k_b.astype(jnp.float32)) * factor
    place = jnp.arange(q_b.shape[0])
    far_ok = (place < anchor_len) & jnp.logical_not(is_anchor)
    own_ok = (place[None, :] <= place[:, None]) & (place[None, :] < length)
    s_far = jnp.where(far_ok[None, None, None, :], s_far, -jnp.inf)
    s_own = jnp.where(own_ok[:, None, None, :], s_own, -jnp.inf)
    top = jnp.maximum(jnp.max(s_far, -1), jnp.max(s_own, -1))
    e_far = jnp.exp(s_far - top[..., None])
    e_own = jnp.exp(s_own - top[..., None])
    total = jnp.sum(e_far, -1) + jnp.sum(e_own, -1)
    summed = jnp.einsum('tgjs,sgd->tgjd', e_far.astype(jnp.bfloat16).astype(jnp.float32), anchor_v.astype(jnp.float32))
    summed = summed + jnp.einsum('tgjs,sgd->tgjd', e_own.astype(jnp.bfloat16).astype(jnp.float32), v_b.astype(jnp.float32))
    return (summed / total[..., None]).astype(jnp.bfloat16)


def question_part(q_rot, k_b, v_b, length):
    factor = HD ** -0.5
    scores = jnp.einsum('rgjd,sgd->rgjs', q_rot.astype(jnp.float32), k_b.astype(jnp.float32)) * factor
    valid = jnp.arange(k_b.shape[0]) < length
    scores = jnp.where(valid[None, None, None, :], scores, -jnp.inf)
    top = jnp.max(scores, -1)
    expo = jnp.exp(scores - top[..., None])
    total = jnp.sum(expo, -1)
    summed = jnp.einsum('rgjs,sgd->rgjd', expo.astype(jnp.bfloat16).astype(jnp.float32), v_b.astype(jnp.float32))
    return top, total, summed


def finish(result, table, length, first):
    count = result.shape[0]
    flat = result.reshape(-1, HD)
    back = jnp.dot(flat, table.astype(jnp.float32), precision=lax.Precision.HIGHEST) * (HD ** -0.5)
    back = back.reshape(count, -1)
    live = (first + jnp.arange(count)) < length
    return jnp.where(live[:, None], back, 0.0).astype(jnp.bfloat16)


def reference(context_q, context_k, context_v, question, block_lengths, anchor_index, question_length):
    blocks = block_lengths.shape[0]
    size = context_q.shape[0] // blocks
    per = QH // KVH
    table = sign_table(HD)
    q_all = context_q.reshape(blocks, size, KVH, per, HD)
    k_all = context_k.reshape(blocks, size, KVH, HD)
    v_all = context_v.reshape(blocks, size, KVH, HD)
    anchor = anchor_index[0]
    anchor_k = lax.dynamic_index_in_dim(k_all, anchor, 0, keepdims=False)
    anchor_v = lax.dynamic_index_in_dim(v_all, anchor, 0, keepdims=False)
    anchor_len = lax.dynamic_index_in_dim(block_lengths, anchor, 0, keepdims=False)

    def one_block(items):
        q_b, k_b, v_b, length, which = items
        out = encode_block(q_b, k_b, v_b, anchor_k, anchor_v, length, anchor_len, which == anchor)
        return out, rotate(k_b, table), rotate(v_b, table)

    outs, k_rot, v_rot = lax.map(one_block, (q_all, k_all, v_all, block_lengths, jnp.arange(blocks, dtype=jnp.int32)))
    mixed = outs.reshape(context_q.shape)
    key_cache = k_rot.reshape(context_k.shape)
    value_cache = v_rot.reshape(context_v.shape)
    q_rot = rotate(question.reshape(QLEN, KVH, per, HD), table)

    def absorb(carry, items):
        top, total, summed = carry
        k_b, v_b, length = items
        part_top, part_total, part_sum = question_part(q_rot, k_b, v_b, length)
        new_top = jnp.maximum(top, part_top)
        old_scale = jnp.exp(top - new_top)
        new_scale = jnp.exp(part_top - new_top)
        return (new_top, total * old_scale + part_total * new_scale,
                summed * old_scale[..., None] + part_sum * new_scale[..., None]), None

    start = (jnp.full((QLEN, KVH, per), -1e30, jnp.float32), jnp.zeros((QLEN, KVH, per), jnp.float32),
             jnp.zeros((QLEN, KVH, per, HD), jnp.float32))
    (top, total, summed), unused = lax.scan(absorb, start, (k_rot, v_rot, block_lengths))
    result = summed / total[..., None]
    answer = finish(result, table, question_length[0], 0)
    return mixed, key_cache, value_cache, answer
```

```python
import functools

import jax
import jax.numpy as jnp
from jax import lax
from jax.experimental import pallas as pl
from jax.experimental.pallas import tpu as pltpu
from jax.sharding import PartitionSpec as P

HD = 128
SC = HD ** (-0.5)
NZ, NY, NC = 8, 4, 2
BLK = 256
BF = jnp.bfloat16
F32 = jnp.float32
SMEM = pl.BlockSpec(memory_space=pltpu.SMEM)
VMEM = pl.BlockSpec(memory_space=pltpu.VMEM)


def index_of(z, y, c):
    return (z * NY + y) * NC + c


def permutation(move):
    return [
        (index_of(z, y, c), index_of(*move(z, y, c)))
        for z in range(NZ)
        for y in range(NY)
        for c in range(NC)
    ]


Z_GROUPS = [[index_of(z, y, c) for z in range(NZ)] for y in range(NY) for c in range(NC)]
OTHER_CORE = permutation(lambda z, y, c: (z, y, 1 - c))
Y_SHIFTS = [permutation(lambda z, y, c, d=d: (z, (y + d) % NY, c)) for d in range(NY)]


def coordinates():
    place = lax.axis_index("ctx")
    return place // (NY * NC), (place // NC) % NY, place % NC


def sign_table():
    shape = (HD, HD)
    both = lax.broadcasted_iota(jnp.int32, shape, 0) & lax.broadcasted_iota(jnp.int32, shape, 1)
    both = both ^ (both >> 4)
    both = both ^ (both >> 2)
    both = both ^ (both >> 1)
    return (1 - 2 * (both & 1)).astype(F32).astype(BF)


def rotated(rows, table):
    return (jnp.dot(rows, table, preferred_element_type=F32) * SC).astype(BF)


def across(a, b):
    return lax.dot_general(a, b, (((1,), (1,)), ((), ())), preferred_element_type=F32)


def prepare_kernel(question_ref, k_ref, v_ref, send_ref, both_ref, rows_ref):
    both_ref[0:BLK, :] = k_ref[...]
    both_ref[BLK : 2 * BLK, :] = v_ref[...]
    question = question_ref[...].astype(F32)
    for k in range(8):
        rows_ref[4 * k : 4 * k + 4, :] = question[:, 256 * k : 256 * k + 256]
    rows = rows_ref[...].astype(BF)
    for z in range(NZ):
        send_ref[z, 0:32, :] = k_ref[32 * z : 32 * z + 32, :]
        send_ref[z, 32:64, :] = v_ref[32 * z : 32 * z + 32, :]
        send_ref[z, 64:96, :] = rows


def prepare(question, k, v):
    return pl.pallas_call(
        prepare_kernel,
        out_shape=(
            jax.ShapeDtypeStruct((NZ, 96, 256), BF),
            jax.ShapeDtypeStruct((2 * BLK, 256), BF),
        ),
        in_specs=[VMEM] * 3,
        out_specs=(VMEM, VMEM),
        scratch_shapes=[pltpu.VMEM((32, 256), F32)],
        name="prepare",
    )(question, k, v)


def question_kernel(lengths_ref, got_ref, *refs):
    blocks, send_ref = refs[:8], refs[8]
    z, y, c = coordinates()
    table = sign_table()
    lane = lax.broadcasted_iota(jnp.int32, (BLK, BLK), 1)
    ids = [index_of(z, lax.rem(y + NY - d, NY), c) for d in range(NY)]
    ids += [index_of(z, lax.rem(y + NY - d, NY), 1 - c) for d in range(NY)]
    stats = []
    for g in range(2):
        halves = [
            got_ref[:, 64 + 16 * g : 80 + 16 * g, HD * half : HD * half + HD].reshape(NZ * 16, HD)
            for half in range(2)
        ]
        q = rotated(jnp.concatenate(halves, axis=0), table)
        top = total = summed = None
        for which in range(8):
            k = rotated(blocks[which][0:BLK, HD * g : HD * g + HD], table)
            v = rotated(blocks[which][BLK : 2 * BLK, HD * g : HD * g + HD], table)
            part = jnp.where(lane < lengths_ref[ids[which]], across(q, k) * SC, -jnp.inf)
            m = jnp.max(part, axis=1, keepdims=True)
            e = jnp.exp(part - m)
            d = jnp.sum(e, axis=1, keepdims=True)
            n = jnp.dot(e.astype(BF), v, preferred_element_type=F32)
            if which == 0:
                top, total, summed = m, d, n
            else:
                new = jnp.maximum(top, m)
                old_scale, scale = jnp.exp(top - new), jnp.exp(m - new)
                top = new
                total = total * old_scale + d * scale
                summed = summed * old_scale + n * scale
        for half in range(2):
            rows = slice(128 * half, 128 * half + 128)
            at = 16 * (2 * g + half)
            send_ref[:, at : at + 16, :] = summed[rows].reshape(NZ, 16, HD)
            stats.append((top[rows], total[rows]))
    lanes = lax.broadcasted_iota(jnp.int32, (HD, HD), 1)
    packed = jnp.zeros((HD, HD), F32)
    for i in range(4):
        packed = jnp.where(lanes == i, stats[i][0], packed)
        packed = jnp.where(lanes == 4 + i, stats[i][1], packed)
    tile = packed.T[0:8, :]
    for i in range(NZ):
        send_ref[i, 64:72, :] = tile


def question_pass(lengths, got, blocks):
    return pl.pallas_call(
        question_kernel,
        out_shape=jax.ShapeDtypeStruct((NZ, 72, HD), F32),
        in_specs=[SMEM] + [VMEM] * 9,
        out_specs=VMEM,
        compiler_params=pltpu.CompilerParams(vmem_limit_bytes=48 * 1024 * 1024),
        cost_estimate=pl.CostEstimate(
            flops=900_000_000, bytes_accessed=2_500_000, transcendentals=1_100_000
        ),
        name="question_pass",
    )(lengths, got, *blocks)


def combine_kernel(anchor_ref, limit_ref, parts_ref, *refs):
    pieces, send_ref, columns_ref = refs[:4], refs[4], refs[5]
    z, y, c = coordinates()
    table = sign_table()
    tiles = [parts_ref[s, 64:72, :] for s in range(NZ)]
    square = jnp.concatenate(tiles + [jnp.zeros((HD - 64, HD), F32)], axis=0)
    columns_ref[...] = square.T
    columns = columns_ref[pl.ds(pl.multiple_of(z * 16, 16), 16), :]
    row = lax.broadcasted_iota(jnp.int32, (64, HD), 0)
    results = []
    for i in range(4):
        tops = [columns[:, 8 * s + i : 8 * s + i + 1] for s in range(NZ)]
        peak = functools.reduce(jnp.maximum, tops)
        total = jnp.zeros((16, 1), F32)
        summed = jnp.zeros((16, HD), F32)
        for s in range(NZ):
            scale = jnp.exp(tops[s] - peak)
            total = total + scale * columns[:, 8 * s + 4 + i : 8 * s + 5 + i]
            summed = summed + scale * parts_ref[s, 16 * i : 16 * i + 16, :]
        results.append(summed / total)
    result = jnp.concatenate(results, axis=0)
    high = result.astype(BF)
    rest = result - high.astype(F32)
    middle = rest.astype(BF)
    low = (rest - middle.astype(F32)).astype(BF)
    back = jnp.dot(low, table, preferred_element_type=F32)
    back = back + jnp.dot(middle, table, preferred_element_type=F32)
    back = (back + jnp.dot(high, table, preferred_element_type=F32)) * SC
    position = index_of(z, y, c) * 4 + (row & 3)
    back = jnp.where(position < limit_ref[0], back, 0.0).astype(BF)
    anchor = anchor_ref[0]
    shift = lax.rem(y + NY - lax.rem(anchor // NC, NY), NY)
    piece = pieces[0][...]
    for d in range(1, NY):
        piece = jnp.where(shift == d, pieces[d][...], piece)
    for i in range(NZ):
        for g in range(2):
            for half in range(2):
                at = 16 * (2 * g + half)
                send_ref[i, 16 * g : 16 * g + 16, HD * half : HD * half + HD] = back[at : at + 16]
        send_ref[i, 32:96, :] = piece


def combine(anchor_index, limit, parts, pieces):
    return pl.pallas_call(
        combine_kernel,
        out_shape=jax.ShapeDtypeStruct((NZ, 96, 256), BF),
        in_specs=[SMEM, SMEM] + [VMEM] * 5,
        out_specs=VMEM,
        scratch_shapes=[pltpu.VMEM((HD, HD), F32)],
        name="combine",
    )(anchor_index, limit, parts, *pieces)


def encode_kernel(anchor_ref, lengths_ref, q_ref, k_ref, v_ref, got_ref, mixed_ref, krot_ref, vrot_ref):
    place = lax.axis_index("ctx")
    anchor = anchor_ref[0]
    k, v = k_ref[...], v_ref[...]

    @pl.when(lax.rem(pl.program_id(0), 8) == 0)
    def _():
        table = sign_table()
        krot_ref[...] = rotated(k, table)
        vrot_ref[...] = rotated(v, table)

    far_k = got_ref[:, 32:64, :].reshape(BLK, HD)
    far_v = got_ref[:, 64:96, :].reshape(BLK, HD)
    q = q_ref[...]
    row = lax.broadcasted_iota(jnp.int32, (BLK, BLK), 0)
    lane = lax.broadcasted_iota(jnp.int32, (BLK, BLK), 1)
    far_len = jnp.where(place == anchor, 0, lengths_ref[anchor])
    s_far = jnp.where(lane < far_len, across(q, far_k) * SC, -jnp.inf)
    own_ok = (lane <= row) & (lane < lengths_ref[place])
    s_own = jnp.where(own_ok, across(q, k) * SC, -jnp.inf)
    top = jnp.max(jnp.maximum(s_far, s_own), axis=1, keepdims=True)
    e_far = jnp.exp(s_far - top)
    e_own = jnp.exp(s_own - top)
    total = jnp.sum(e_far + e_own, axis=1, keepdims=True)
    summed = jnp.dot(e_far.astype(BF), far_v, preferred_element_type=F32)
    summed = summed + jnp.dot(e_own.astype(BF), v, preferred_element_type=F32)
    mixed_ref[...] = (summed / total).astype(BF)


def encode(anchor_index, lengths, q, k, v, got):
    head = pl.BlockSpec((BLK, HD), lambda h: (0, h))
    group = pl.BlockSpec((BLK, HD), lambda h: (0, h // 8))
    return pl.pallas_call(
        encode_kernel,
        grid=(16,),
        out_shape=(
            jax.ShapeDtypeStruct(q.shape, BF),
            jax.ShapeDtypeStruct(k.shape, BF),
            jax.ShapeDtypeStruct(v.shape, BF),
        ),
        in_specs=[
            SMEM,
            SMEM,
            head,
            group,
            group,
            pl.BlockSpec((NZ, 96, HD), lambda h: (0, 0, h // 8)),
        ],
        out_specs=(head, group, group),
        cost_estimate=pl.CostEstimate(
            flops=1_100_000_000, bytes_accessed=3_500_000, transcendentals=2_100_000
        ),
        name="encode",
    )(anchor_index, lengths, q, k, v, got)


def assemble_kernel(*refs):
    own, other, out_ref = refs[0:4], refs[4:8], refs[8]
    z, y, c = coordinates()
    upper = lax.broadcasted_iota(jnp.int32, (8, 256), 0) < 4
    for d in range(NY):
        at = lax.rem(y + NY - d, NY)
        mine = own[d][0].astype(F32)
        theirs = other[d][0].astype(F32)
        first = jnp.where(c == 0, mine, theirs)
        second = jnp.where(c == 0, theirs, mine)
        for m in range(4):
            a, b = first[8 * m : 8 * m + 8], second[8 * m : 8 * m + 8]
            even = jnp.where(upper, a, pltpu.roll(b, 4, 0))
            odd = jnp.where(upper, pltpu.roll(a, 4, 0), b)
            out_ref[0, at, :, 512 * m : 512 * m + 256] = even.astype(BF)
            out_ref[0, at, :, 512 * m + 256 : 512 * m + 512] = odd.astype(BF)


def assemble(own, other):
    part = pl.BlockSpec((1, 32, 256), lambda i: (i, 0, 0))
    return pl.pallas_call(
        assemble_kernel,
        grid=(NZ,),
        out_shape=jax.ShapeDtypeStruct((NZ, NY, 8, 2048), BF),
        in_specs=[part] * 8,
        out_specs=pl.BlockSpec((1, NY, 8, 2048), lambda i: (i, 0, 0, 0)),
        name="assemble",
    )(*own, *other)


def on_device(
    context_q, context_k, context_v, question, block_lengths, anchor_index, question_length
):
    def swap(x):
        return lax.ppermute(x, "ctx", OTHER_CORE)

    def along_y(x):
        return [x] + [lax.ppermute(x, "ctx", Y_SHIFTS[d]) for d in range(1, NY)]

    def over_z(x):
        return lax.all_to_all(x, "ctx", 0, 0, axis_index_groups=Z_GROUPS)

    send, both = prepare(question, context_k, context_v)
    blocks = along_y(both)
    got = over_z(send)
    blocks = blocks + [swap(b) for b in blocks]
    anchor = anchor_index[0]
    piece = lax.dynamic_index_in_dim(got[:, 0:64, :], anchor // (NY * NC), 0, keepdims=False)
    core = lax.axis_index("ctx") % NC
    piece = jnp.where(anchor % NC == core, piece, swap(piece))
    pieces = along_y(piece)
    parts = over_z(question_pass(block_lengths, got, blocks))
    final = over_z(combine(anchor_index, question_length, parts, pieces))
    own = along_y(final[:, 0:32, :])
    mixed, key_cache, value_cache = encode(
        anchor_index, block_lengths, context_q, context_k, context_v, final
    )
    other = [swap(x) for x in own]
    answer = assemble(own, other).reshape(256, 2048)
    return mixed, key_cache, value_cache, answer


def solution(mesh):
    placed = (
        P("ctx", "heads"),
        P("ctx", "heads"),
        P("ctx", "heads"),
        P("ctx", "heads"),
        P(),
        P(),
        P(),
    )
    return jax.shard_map(
        on_device,
        mesh=mesh,
        in_specs=placed,
        out_specs=(P("ctx", "heads"), P("ctx", "heads"), P("ctx", "heads"), P(None, "heads")),
        check_vma=False,
    )
```

```python
import functools
import math

import jax
import jax.numpy as jnp
from jax import lax
from jax.experimental import pallas as pl
from jax.experimental.pallas import tpu as pltpu
from jax.sharding import PartitionSpec as P

HD = 128
SC = HD ** (-0.5)
SC2 = SC * math.log2(math.e)
NZ, NY, NC = 8, 4, 2
BLK = 256
BF = jnp.bfloat16
F32 = jnp.float32
SMEM = pl.BlockSpec(memory_space=pltpu.SMEM)
VMEM = pl.BlockSpec(memory_space=pltpu.VMEM)
PARAMS = pltpu.CompilerParams(vmem_limit_bytes=20 * 1024 * 1024)


def index_of(z, y, c):
    return (z * NY + y) * NC + c


def permutation(move):
    return [
        (index_of(z, y, c), index_of(*move(z, y, c)))
        for z in range(NZ)
        for y in range(NY)
        for c in range(NC)
    ]


Z_GROUPS = [[index_of(z, y, c) for z in range(NZ)] for y in range(NY) for c in range(NC)]
CHIP_GROUPS = [[index_of(z, y, c) for z in range(NZ) for y in range(NY)] for c in range(NC)]
OTHER_CORE = permutation(lambda z, y, c: (z, y, 1 - c))
Y_SHIFTS = [permutation(lambda z, y, c, d=d: (z, (y + d) % NY, c)) for d in range(NY)]
Z_SHIFTS = [permutation(lambda z, y, c, d=d: ((z + d) % NZ, y, c)) for d in range(NZ)]


def coordinates():
    place = lax.axis_index("ctx")
    return place // (NY * NC), (place // NC) % NY, place % NC


def sign_table():
    shape = (HD, HD)
    both = lax.broadcasted_iota(jnp.int32, shape, 0) & lax.broadcasted_iota(jnp.int32, shape, 1)
    both = both ^ (both >> 4)
    both = both ^ (both >> 2)
    both = both ^ (both >> 1)
    return (1 - 2 * (both & 1)).astype(F32).astype(BF)


def across(a, b):
    return lax.dot_general(a, b, (((1,), (1,)), ((), ())), preferred_element_type=F32)


def dot(a, b):
    return jnp.dot(a, b, preferred_element_type=F32)


def rotated(rows, table):
    return (dot(rows, table) * SC).astype(BF)


def join_kernel(k_ref, v_ref, both_ref, sems):
    copies = [
        pltpu.make_async_copy(k_ref, both_ref.at[0:BLK, :], sems.at[0]),
        pltpu.make_async_copy(v_ref, both_ref.at[BLK : 2 * BLK, :], sems.at[1]),
    ]
    for copy in copies:
        copy.start()
    for copy in copies:
        copy.wait()


def join(k, v):
    return pl.pallas_call(
        join_kernel,
        out_shape=jax.ShapeDtypeStruct((2 * BLK, 256), BF),
        in_specs=[pl.BlockSpec(memory_space=pl.ANY)] * 2,
        out_specs=VMEM,
        scratch_shapes=[pltpu.SemaphoreType.DMA((2,))],
        name="join",
    )(k, v)


def repeat_kernel(question_ref, send_ref, scratch_ref):
    question = question_ref[...].astype(F32)
    for k in range(8):
        scratch_ref[4 * k : 4 * k + 4, :] = question[:, 256 * k : 256 * k + 256]
    rows = scratch_ref[...].astype(BF)
    for i in range(NZ):
        send_ref[i] = rows


def repeat(question):
    return pl.pallas_call(
        repeat_kernel,
        out_shape=jax.ShapeDtypeStruct((NZ, 32, 256), BF),
        in_specs=[VMEM],
        out_specs=VMEM,
        scratch_shapes=[pltpu.VMEM((32, 256), F32)],
        name="repeat",
    )(question)


def gate_kernel(*refs):
    pass


def gate(arrays, token):
    anywhere = pl.BlockSpec(memory_space=pl.ANY)
    return pl.pallas_call(
        gate_kernel,
        out_shape=[jax.ShapeDtypeStruct(x.shape, x.dtype) for x in arrays],
        in_specs=[anywhere] * (len(arrays) + 1),
        out_specs=[anywhere] * len(arrays),
        input_output_aliases={i: i for i in range(len(arrays))},
        compiler_params=pltpu.CompilerParams(vmem_limit_bytes=1024 * 1024),
        name="gate",
    )(*arrays, token)


def pick_kernel(anchor_ref, *refs):
    blocks, out_ref, sems = refs[:8], refs[8], refs[9]
    z, y, c = coordinates()
    wanted = lax.rem(anchor_ref[0], NY * NC)
    first = pl.multiple_of(64 * y, 64)
    for which in range(8):
        core = c if which < NY else 1 - c
        place = NC * lax.rem(y + NY - which % NY, NY) + core

        @pl.when(place == wanted)
        def _(which=which):
            copies = [
                pltpu.make_async_copy(
                    blocks[which].at[pl.ds(first + BLK * i, 64), :],
                    out_ref.at[64 * i : 64 * i + 64, :],
                    sems.at[i],
                )
                for i in range(2)
            ]
            for copy in copies:
                copy.start()
            for copy in copies:
                copy.wait()


def pick(anchor_index, blocks):
    anywhere = pl.BlockSpec(memory_space=pl.ANY)
    return pl.pallas_call(
        pick_kernel,
        out_shape=jax.ShapeDtypeStruct((HD, 256), BF),
        in_specs=[SMEM] + [anywhere] * 8,
        out_specs=VMEM,
        scratch_shapes=[pltpu.SemaphoreType.DMA((2,))],
        compiler_params=pltpu.CompilerParams(vmem_limit_bytes=1024 * 1024),
        name="pick",
    )(anchor_index, *blocks)


def thirds(x):
    high = x.astype(BF)
    rest = x - high.astype(F32)
    middle = rest.astype(BF)
    return high, middle, (rest - middle.astype(F32)).astype(BF)


def question_kernel(lengths_ref, got_ref, *refs):
    blocks, send_ref = refs[:8], refs[8]
    z, y, c = coordinates()
    table = sign_table()
    lane = lax.broadcasted_iota(jnp.int32, (BLK, BLK), 1)
    ids = [index_of(z, lax.rem(y + NY - d, NY), c) for d in range(NY)]
    ids += [index_of(z, lax.rem(y + NY - d, NY), 1 - c) for d in range(NY)]
    stats = []
    for g in range(2):
        lanes = slice(HD * g, HD * g + HD)
        halves = [
            got_ref[:, 16 * g : 16 * g + 16, HD * half : HD * half + HD].reshape(NZ * 16, HD)
            for half in range(2)
        ]
        q = rotated(jnp.concatenate(halves, axis=0), table)
        top = total = summed = None
        for which in range(8):
            k = rotated(blocks[which][0:BLK, lanes], table)
            v = rotated(blocks[which][BLK : 2 * BLK, lanes], table)
            part = jnp.where(lane < lengths_ref[ids[which]], across(q, k) * SC2, -jnp.inf)
            m = jnp.max(part, axis=1, keepdims=True)
            e = jnp.exp2(part - m)
            d = jnp.sum(e, axis=1, keepdims=True)
            n = dot(e.astype(BF), v)
            if which == 0:
                top, total, summed = m, d, n
            else:
                new = jnp.maximum(top, m)
                old_scale, scale = jnp.exp2(top - new), jnp.exp2(m - new)
                top = new
                total = total * old_scale + d * scale
                summed = summed * old_scale + n * scale
        for half in range(2):
            rows = slice(HD * half, HD * half + HD)
            at = 16 * (2 * g + half)
            send_ref[:, at : at + 16, :] = summed[rows].reshape(NZ, 16, HD)
            stats.append((top[rows], total[rows]))
    lanes = lax.broadcasted_iota(jnp.int32, (HD, HD), 1)
    packed = jnp.zeros((HD, HD), F32)
    for i in range(4):
        packed = jnp.where(lanes == i, stats[i][0], packed)
        packed = jnp.where(lanes == 4 + i, stats[i][1], packed)
    tile = packed.T[0:8, :]
    for i in range(NZ):
        send_ref[i, 64:72, :] = tile


def question_pass(lengths, got, blocks):
    return pl.pallas_call(
        question_kernel,
        out_shape=jax.ShapeDtypeStruct((NZ, 72, HD), F32),
        in_specs=[SMEM] + [VMEM] * 9,
        out_specs=VMEM,
        compiler_params=PARAMS,
        cost_estimate=pl.CostEstimate(
            flops=900_000_000, bytes_accessed=2_500_000, transcendentals=1_100_000
        ),
        name="question_pass",
    )(lengths, got, *blocks)


def combine_kernel(limit_ref, parts_ref, piece_ref, send_ref, columns_ref):
    z, y, c = coordinates()
    table = sign_table()
    tiles = [parts_ref[s, 64:72, :] for s in range(NZ)]
    square = jnp.concatenate(tiles + [jnp.zeros((HD - 64, HD), F32)], axis=0)
    columns_ref[...] = square.T
    columns = columns_ref[pl.ds(pl.multiple_of(z * 16, 16), 16), :]
    row = lax.broadcasted_iota(jnp.int32, (64, HD), 0)
    results = []
    for i in range(4):
        tops = [columns[:, 8 * s + i : 8 * s + i + 1] for s in range(NZ)]
        peak = functools.reduce(jnp.maximum, tops)
        total = jnp.zeros((16, 1), F32)
        summed = jnp.zeros((16, HD), F32)
        for s in range(NZ):
            scale = jnp.exp2(tops[s] - peak)
            total = total + scale * columns[:, 8 * s + 4 + i : 8 * s + 5 + i]
            summed = summed + scale * parts_ref[s, 16 * i : 16 * i + 16, :]
        results.append(summed / total)
    high, middle, low = thirds(jnp.concatenate(results, axis=0))
    back = (dot(low, table) + dot(middle, table) + dot(high, table)) * SC
    position = index_of(z, y, c) * 4 + (row & 3)
    back = jnp.where(position < limit_ref[0], back, 0.0).astype(BF)
    for i in range(NZ * NY):
        send_ref[i] = back


def combine(limit, parts, piece):
    return pl.pallas_call(
        combine_kernel,
        out_shape=jax.ShapeDtypeStruct((NZ * NY, 64, HD), BF),
        in_specs=[SMEM, VMEM, pl.BlockSpec(memory_space=pl.ANY)],
        out_specs=VMEM,
        scratch_shapes=[pltpu.VMEM((HD, HD), F32)],
        compiler_params=PARAMS,
        name="combine",
    )(limit, parts, piece)


def encode_kernel(anchor_ref, lengths_ref, q_ref, k_ref, v_ref, *refs):
    pieces = refs[:NY]
    mixed_ref, krot_ref, vrot_ref, far_k_ref, far_v_ref = refs[NY:]
    z, y, c = coordinates()
    place = index_of(z, y, c)
    anchor = anchor_ref[0]
    k, v = k_ref[...], v_ref[...]
    table = sign_table()
    krot_ref[...] = rotated(k, table)
    vrot_ref[...] = rotated(v, table)
    for d in range(NY):
        at = pl.multiple_of(64 * lax.rem(y + NY - d, NY), 64)
        far_k_ref[pl.ds(at, 64), :] = pieces[d][0:64, :]
        far_v_ref[pl.ds(at, 64), :] = pieces[d][64:128, :]
    far_k, far_v = far_k_ref[...], far_v_ref[...]
    far_len = jnp.where(place == anchor, 0, lengths_ref[anchor])
    own_len = lengths_ref[place]
    query = lax.broadcasted_iota(jnp.int32, (BLK, BLK), 0)
    key = lax.broadcasted_iota(jnp.int32, (BLK, BLK), 1)
    far_ok = key < far_len
    own_ok = (key <= query) & (key < own_len)
    for j in range(8):
        q = q_ref[:, HD * j : HD * j + HD]
        s_far = jnp.where(far_ok, across(q, far_k) * SC2, -jnp.inf)
        s_own = jnp.where(own_ok, across(q, k) * SC2, -jnp.inf)
        top = jnp.max(jnp.maximum(s_far, s_own), axis=1, keepdims=True)
        e_far = jnp.exp2(s_far - top)
        e_own = jnp.exp2(s_own - top)
        total = jnp.sum(e_far + e_own, axis=1, keepdims=True)
        summed = dot(e_far.astype(BF), far_v) + dot(e_own.astype(BF), v)
        mixed_ref[:, HD * j : HD * j + HD] = (summed / total).astype(BF)


def encode(anchor_index, lengths, q, k, v, pieces):
    heads = pl.BlockSpec((BLK, 8 * HD), lambda g: (0, g))
    group = pl.BlockSpec((BLK, HD), lambda g: (0, g))
    piece = pl.BlockSpec((HD, HD), lambda g: (0, g))
    return pl.pallas_call(
        encode_kernel,
        grid=(2,),
        out_shape=(
            jax.ShapeDtypeStruct(q.shape, BF),
            jax.ShapeDtypeStruct(k.shape, BF),
            jax.ShapeDtypeStruct(v.shape, BF),
        ),
        in_specs=[SMEM, SMEM, heads, group, group] + [piece] * NY,
        out_specs=(heads, group, group),
        scratch_shapes=[pltpu.VMEM((BLK, HD), BF), pltpu.VMEM((BLK, HD), BF)],
        compiler_params=PARAMS,
        cost_estimate=pl.CostEstimate(
            flops=1_100_000_000, bytes_accessed=3_500_000, transcendentals=2_100_000
        ),
        name="encode",
    )(anchor_index, lengths, q, k, v, *pieces)


def assemble_kernel(own_ref, other_ref, out_ref):
    c = coordinates()[2]
    upper = lax.broadcasted_iota(jnp.int32, (8, HD), 0) < 4
    for pair in range(4):
        sources = []
        for i in (2 * pair, 2 * pair + 1):
            mine = own_ref[i].astype(F32)
            theirs = other_ref[i].astype(F32)
            sources.append((jnp.where(c == 0, mine, theirs), jnp.where(c == 0, theirs, mine)))
        for at in range(8):
            evens, odds = [], []
            for first, second in sources:
                a, b = first[8 * at : 8 * at + 8], second[8 * at : 8 * at + 8]
                evens.append(jnp.where(upper, a, pltpu.roll(b, 4, 0)))
                odds.append(jnp.where(upper, pltpu.roll(a, 4, 0), b))
            g, half, pair_of = at // 4, at // 2 % 2, at % 2
            head = 8 * g + 4 * pair_of + half
            rows = slice(16 * pair, 16 * pair + 16)
            out_ref[rows, HD * head : HD * head + HD] = jnp.concatenate(evens, axis=0).astype(BF)
            head = head + 2
            out_ref[rows, HD * head : HD * head + HD] = jnp.concatenate(odds, axis=0).astype(BF)


def assemble(own, other):
    part = pl.BlockSpec((8, 64, HD), lambda i: (i, 0, 0))
    return pl.pallas_call(
        assemble_kernel,
        grid=(4,),
        out_shape=jax.ShapeDtypeStruct((256, 2048), BF),
        in_specs=[part] * 2,
        out_specs=pl.BlockSpec((64, 2048), lambda i: (i, 0)),
        compiler_params=PARAMS,
        name="assemble",
    )(own, other)


def on_device(
    context_q, context_k, context_v, question, block_lengths, anchor_index, question_length
):
    def swap(x):
        return lax.ppermute(x, "ctx", OTHER_CORE)

    def along_y(x):
        return [x] + [lax.ppermute(x, "ctx", Y_SHIFTS[d]) for d in range(1, NY)]

    def along_z(x, d):
        return lax.ppermute(x, "ctx", Z_SHIFTS[d]), lax.ppermute(x, "ctx", Z_SHIFTS[NZ - d])

    def with_other_core(parts):
        return parts + [swap(x) for x in parts]

    both = join(context_k, context_v)
    blocks = along_y(both)
    got = lax.all_to_all(repeat(question), "ctx", 0, 0, axis_index_groups=Z_GROUPS)
    blocks = with_other_core([both, *gate(blocks[1:], got)])
    piece = pick(anchor_index, blocks)
    below, above = along_z(piece, 1)
    send = question_pass(block_lengths, got, blocks)
    parts = lax.all_to_all(send, "ctx", 0, 0, axis_index_groups=Z_GROUPS)
    distance = (lax.axis_index("ctx") // (NY * NC) - anchor_index[0] // (NY * NC)) & (NZ - 1)
    piece = jnp.where(distance == 1, below, jnp.where(distance == NZ - 1, above, piece))
    below, above = along_z(piece, 3)
    near = (distance < 2) | (distance == NZ - 1)
    piece = jnp.where(near, piece, jnp.where(distance < 5, below, above))
    spread = combine(question_length, parts, piece)
    own = lax.all_to_all(spread, "ctx", 0, 0, axis_index_groups=CHIP_GROUPS)
    mixed, key_cache, value_cache = encode(
        anchor_index, block_lengths, context_q, context_k, context_v, along_y(piece)
    )
    (own,) = gate([own], key_cache)
    answer = assemble(own, swap(own))
    return mixed, key_cache, value_cache, answer


def solution(mesh):
    placed = (
        P("ctx", "heads"),
        P("ctx", "heads"),
        P("ctx", "heads"),
        P("ctx", "heads"),
        P(),
        P(),
        P(),
    )
    return jax.shard_map(
        on_device,
        mesh=mesh,
        in_specs=placed,
        out_specs=(P("ctx", "heads"), P("ctx", "heads"), P("ctx", "heads"), P(None, "heads")),
        check_vma=False,
    )
```

```python
import functools
import math

import jax
import jax.numpy as jnp
from jax import lax
from jax.experimental import pallas as pl
from jax.experimental.pallas import tpu as pltpu
from jax.sharding import PartitionSpec as P

HD = 128
SC = HD ** (-0.5)
SC2 = SC * math.log2(math.e)
NZ, NY, NC = 8, 4, 2
BLK = 256
BF = jnp.bfloat16
F32 = jnp.float32
SMEM = pl.BlockSpec(memory_space=pltpu.SMEM)
VMEM = pl.BlockSpec(memory_space=pltpu.VMEM)
SMALL = pltpu.CompilerParams(vmem_limit_bytes=4 * 1024 * 1024)
PARAMS = pltpu.CompilerParams(vmem_limit_bytes=20 * 1024 * 1024)


def index_of(z, y, c):
    return (z * NY + y) * NC + c


def permutation(move):
    return [
        (index_of(z, y, c), index_of(*move(z, y, c)))
        for z in range(NZ)
        for y in range(NY)
        for c in range(NC)
    ]


Z_GROUPS = [[index_of(z, y, c) for z in range(NZ)] for y in range(NY) for c in range(NC)]
CHIP_GROUPS = [[index_of(z, y, c) for z in range(NZ) for y in range(NY)] for c in range(NC)]
OTHER_CORE = permutation(lambda z, y, c: (z, y, 1 - c))
Y_SHIFTS = [permutation(lambda z, y, c, d=d: (z, (y + d) % NY, c)) for d in range(NY)]
Z_SHIFTS = [permutation(lambda z, y, c, d=d: ((z + d) % NZ, y, c)) for d in range(NZ)]


def coordinates():
    place = lax.axis_index("ctx")
    return place // (NY * NC), (place // NC) % NY, place % NC


def sign_table():
    shape = (HD, HD)
    both = lax.broadcasted_iota(jnp.int32, shape, 0) & lax.broadcasted_iota(jnp.int32, shape, 1)
    both = both ^ (both >> 4)
    both = both ^ (both >> 2)
    both = both ^ (both >> 1)
    return (1 - 2 * (both & 1)).astype(F32).astype(BF)


def across(a, b):
    return lax.dot_general(a, b, (((1,), (1,)), ((), ())), preferred_element_type=F32)


def dot(a, b):
    return jnp.dot(a, b, preferred_element_type=F32)


def rotated(rows, table):
    return (dot(rows, table) * SC).astype(BF)


def join_kernel(k_ref, v_ref, k_other_ref, v_other_ref, both_ref):
    c = coordinates()[2]
    for head in range(NC):

        @pl.when(c == head)
        def _(head=head):
            lanes = slice(HD * head, HD * head + HD)
            for i, source in enumerate((k_ref, v_ref, k_other_ref, v_other_ref)):
                both_ref[BLK * i : BLK * i + BLK, :] = source[:, lanes]


def join(k, v, k_other, v_other):
    return pl.pallas_call(
        join_kernel,
        out_shape=jax.ShapeDtypeStruct((4 * BLK, HD), BF),
        in_specs=[VMEM] * 4,
        out_specs=VMEM,
        compiler_params=SMALL,
        name="join",
    )(k, v, k_other, v_other)


def repeat_kernel(own_ref, other_ref, send_ref, rows_ref):
    c = coordinates()[2]
    own, other = own_ref[...].astype(F32), other_ref[...].astype(F32)
    first, second = jnp.where(c == 0, own, other), jnp.where(c == 0, other, own)
    for at, source in enumerate((first, second)):
        for j in range(8):
            left, right = source[:, HD * j : HD * j + HD], source[:, HD * (8 + j) : HD * (9 + j)]
            rows_ref[8 * j + 4 * at : 8 * j + 4 * at + 4, :] = jnp.where(c == 0, left, right)
    rows = rows_ref[...].astype(BF)
    for i in range(NZ):
        send_ref[i] = rows


def repeat(own, other):
    return pl.pallas_call(
        repeat_kernel,
        out_shape=jax.ShapeDtypeStruct((NZ, 64, HD), BF),
        in_specs=[VMEM] * 2,
        out_specs=VMEM,
        scratch_shapes=[pltpu.VMEM((64, HD), F32)],
        compiler_params=SMALL,
        name="repeat",
    )(own, other)


def gate_kernel(*refs):
    pass


def gate(arrays, token):
    anywhere = pl.BlockSpec(memory_space=pl.ANY)
    return pl.pallas_call(
        gate_kernel,
        out_shape=[jax.ShapeDtypeStruct(x.shape, x.dtype) for x in arrays],
        in_specs=[anywhere] * (len(arrays) + 1),
        out_specs=[anywhere] * len(arrays),
        input_output_aliases={i: i for i in range(len(arrays))},
        compiler_params=pltpu.CompilerParams(vmem_limit_bytes=1024 * 1024),
        name="gate",
    )(*arrays, token)


def pick_kernel(anchor_ref, *refs):
    columns, out_ref, sems = refs[:NY], refs[NY], refs[NY + 1]
    z, y, c = coordinates()
    wanted = lax.rem(anchor_ref[0], NY * NC)
    rows = HD * lax.rem(y, 2)
    for which in range(8):
        core = c if which < NY else 1 - c
        place = NC * lax.rem(y + NY - which % NY, NY) + core

        @pl.when(place == wanted)
        def _(which=which):
            copies = []
            for i in range(2):
                first = pl.multiple_of(2 * BLK * (which // NY) + BLK * i + rows, HD)
                source = columns[which % NY].at[pl.ds(first, HD), :]
                target = out_ref.at[HD * i : HD * i + HD, :]
                copies.append(pltpu.make_async_copy(source, target, sems.at[i]))
            for copy in copies:
                copy.start()
            for copy in copies:
                copy.wait()


def pick(anchor_index, columns):
    anywhere = pl.BlockSpec(memory_space=pl.ANY)
    return pl.pallas_call(
        pick_kernel,
        out_shape=jax.ShapeDtypeStruct((BLK, HD), BF),
        in_specs=[SMEM] + [anywhere] * NY,
        out_specs=VMEM,
        scratch_shapes=[pltpu.SemaphoreType.DMA((2,))],
        compiler_params=pltpu.CompilerParams(vmem_limit_bytes=1024 * 1024),
        name="pick",
    )(anchor_index, *columns)


def thirds(x):
    high = x.astype(BF)
    rest = x - high.astype(F32)
    middle = rest.astype(BF)
    return high, middle, (rest - middle.astype(F32)).astype(BF)


def question_kernel(lengths_ref, got_ref, *refs):
    columns, send_ref = refs[:NY], refs[NY]
    z, y, c = coordinates()
    table = sign_table()
    lane = lax.broadcasted_iota(jnp.int32, (BLK, BLK), 1)
    ids = [index_of(z, lax.rem(y + NY - d, NY), c) for d in range(NY)]
    ids += [index_of(z, lax.rem(y + NY - d, NY), 1 - c) for d in range(NY)]
    q = rotated(got_ref[...].reshape(NZ * 64, HD), table)
    halves = [q[0:BLK], q[BLK : 2 * BLK]]
    tops, totals, sums = [None] * 2, [None] * 2, [None] * 2
    for which in range(8):
        column, first = columns[which % NY], 2 * BLK * (which // NY)
        k = rotated(column[first : first + BLK, :], table)
        v = rotated(column[first + BLK : first + 2 * BLK, :], table)
        ok = lane < lengths_ref[ids[which]]
        for i in range(2):
            part = jnp.where(ok, across(halves[i], k) * SC2, -jnp.inf)
            m = jnp.max(part, axis=1, keepdims=True)
            e = jnp.exp2(part - m)
            d = jnp.sum(e, axis=1, keepdims=True)
            n = dot(e.astype(BF), v)
            if which == 0:
                tops[i], totals[i], sums[i] = m, d, n
            else:
                new = jnp.maximum(tops[i], m)
                old_scale, scale = jnp.exp2(tops[i] - new), jnp.exp2(m - new)
                tops[i] = new
                totals[i] = totals[i] * old_scale + d * scale
                sums[i] = sums[i] * old_scale + n * scale
    lanes = lax.broadcasted_iota(jnp.int32, (HD, HD), 1)
    packed = jnp.zeros((HD, HD), F32)
    for i in range(4):
        rows = slice(HD * (i % 2), HD * (i % 2) + HD)
        packed = jnp.where(lanes == i, tops[i // 2][rows], packed)
        packed = jnp.where(lanes == 4 + i, totals[i // 2][rows], packed)
    tile = packed.T[0:8, :]
    for i in range(2):
        send_ref[4 * i : 4 * i + 4, 0:64, :] = sums[i].reshape(4, 64, HD)
    for i in range(NZ):
        send_ref[i, 64:72, :] = tile


def question_pass(lengths, got, columns):
    return pl.pallas_call(
        question_kernel,
        out_shape=jax.ShapeDtypeStruct((NZ, 72, HD), F32),
        in_specs=[SMEM] + [VMEM] * (1 + NY),
        out_specs=VMEM,
        compiler_params=PARAMS,
        cost_estimate=pl.CostEstimate(
            flops=900_000_000, bytes_accessed=2_500_000, transcendentals=1_100_000
        ),
        name="question_pass",
    )(lengths, got, *columns)


def combine_kernel(limit_ref, parts_ref, piece_ref, send_ref, columns_ref):
    z, y, c = coordinates()
    table = sign_table()
    tops = [parts_ref[s, pl.ds(64 + z // 2, 1), :] for s in range(NZ)]
    totals = [parts_ref[s, pl.ds(68 + z // 2, 1), :] for s in range(NZ)]
    square = jnp.concatenate(tops + totals + [jnp.zeros((HD - 16, HD), F32)], axis=0)
    columns_ref[...] = square.T
    columns = columns_ref[pl.ds(pl.multiple_of(z % 2 * 64, 64), 64), :]
    row = lax.broadcasted_iota(jnp.int32, (64, HD), 0)
    tops = [columns[:, s : s + 1] for s in range(NZ)]
    peak = functools.reduce(jnp.maximum, tops)
    total = jnp.zeros((64, 1), F32)
    summed = jnp.zeros((64, HD), F32)
    for s in range(NZ):
        scale = jnp.exp2(tops[s] - peak)
        total = total + scale * columns[:, NZ + s : NZ + s + 1]
        summed = summed + scale * parts_ref[s, 0:64, :]
    high, middle, low = thirds(summed / total)
    back = (dot(low, table) + dot(middle, table) + dot(high, table)) * SC
    position = (z * NY + y) * 8 + (row & 7)
    back = jnp.where(position < limit_ref[0], back, 0.0).astype(BF)
    for i in range(NZ * NY):
        send_ref[i] = back


def combine(limit, parts, piece):
    return pl.pallas_call(
        combine_kernel,
        out_shape=jax.ShapeDtypeStruct((NZ * NY, 64, HD), BF),
        in_specs=[SMEM, VMEM, pl.BlockSpec(memory_space=pl.ANY)],
        out_specs=VMEM,
        scratch_shapes=[pltpu.VMEM((HD, HD), F32)],
        compiler_params=SMALL,
        name="combine",
    )(limit, parts, piece)


def encode_kernel(anchor_ref, lengths_ref, q_ref, k_ref, v_ref, *refs):
    pieces = refs[:4]
    mixed_ref, krot_ref, vrot_ref, token_ref, far_k_ref, far_v_ref = refs[4:]
    z, y, c = coordinates()
    place = index_of(z, y, c)
    anchor = anchor_ref[0]
    k, v = k_ref[...], v_ref[...]
    table = sign_table()
    krot_ref[...] = rotated(k, table)
    vrot_ref[...] = rotated(v, table)
    token_ref[...] = jnp.zeros_like(token_ref)
    g = pl.program_id(0)
    for core in range(2):

        @pl.when((g == c) == (core == 0))
        def _(core=core):
            for i in range(2):
                at = pl.multiple_of(HD * lax.rem(y + i, 2), HD)
                far_k_ref[pl.ds(at, HD), :] = pieces[2 * core + i][0:HD, :]
                far_v_ref[pl.ds(at, HD), :] = pieces[2 * core + i][HD : 2 * HD, :]

    far_k, far_v = far_k_ref[...], far_v_ref[...]
    far_len = jnp.where(place == anchor, 0, lengths_ref[anchor])
    own_len = lengths_ref[place]
    query = lax.broadcasted_iota(jnp.int32, (BLK, BLK), 0)
    key = lax.broadcasted_iota(jnp.int32, (BLK, BLK), 1)
    far_ok = key < far_len
    own_ok = (key <= query) & (key < own_len)
    for j in range(8):
        q = q_ref[:, HD * j : HD * j + HD]
        s_far = jnp.where(far_ok, across(q, far_k) * SC2, -jnp.inf)
        s_own = jnp.where(own_ok, across(q, k) * SC2, -jnp.inf)
        top = jnp.max(jnp.maximum(s_far, s_own), axis=1, keepdims=True)
        e_far = jnp.exp2(s_far - top)
        e_own = jnp.exp2(s_own - top)
        total = jnp.sum(e_far + e_own, axis=1, keepdims=True)
        summed = dot(e_far.astype(BF), far_v) + dot(e_own.astype(BF), v)
        mixed_ref[:, HD * j : HD * j + HD] = (summed / total).astype(BF)


def encode(anchor_index, lengths, q, k, v, pieces):
    heads = pl.BlockSpec((BLK, 8 * HD), lambda g: (0, g))
    group = pl.BlockSpec((BLK, HD), lambda g: (0, g))
    token = pl.BlockSpec((8, HD), lambda g: (0, 0))
    return pl.pallas_call(
        encode_kernel,
        grid=(2,),
        out_shape=(
            jax.ShapeDtypeStruct(q.shape, BF),
            jax.ShapeDtypeStruct(k.shape, BF),
            jax.ShapeDtypeStruct(v.shape, BF),
            jax.ShapeDtypeStruct((8, HD), F32),
        ),
        in_specs=[SMEM, SMEM, heads, group, group] + [VMEM] * 4,
        out_specs=(heads, group, group, token),
        scratch_shapes=[pltpu.VMEM((BLK, HD), BF), pltpu.VMEM((BLK, HD), BF)],
        compiler_params=PARAMS,
        cost_estimate=pl.CostEstimate(
            flops=1_100_000_000, bytes_accessed=3_500_000, transcendentals=2_100_000
        ),
        name="encode",
    )(anchor_index, lengths, q, k, v, *pieces)


def assemble_kernel(own_ref, other_ref, out_ref):
    c = coordinates()[2]
    for pair in range(4):
        sources = []
        for i in (2 * pair, 2 * pair + 1):
            own, other = own_ref[i].astype(F32), other_ref[i].astype(F32)
            sources.append((jnp.where(c == 0, own, other), jnp.where(c == 0, other, own)))
        rows = slice(16 * pair, 16 * pair + 16)
        for g in range(2):
            for j in range(8):
                parts = [source[g][8 * j : 8 * j + 8] for source in sources]
                lanes = slice(HD * (8 * g + j), HD * (8 * g + j) + HD)
                out_ref[rows, lanes] = jnp.concatenate(parts, axis=0).astype(BF)


def assemble(own, other):
    part = pl.BlockSpec((8, 64, HD), lambda i: (i, 0, 0))
    return pl.pallas_call(
        assemble_kernel,
        grid=(4,),
        out_shape=jax.ShapeDtypeStruct((256, 2048), BF),
        in_specs=[part] * 2,
        out_specs=pl.BlockSpec((64, 2048), lambda i: (i, 0)),
        compiler_params=PARAMS,
        name="assemble",
    )(own, other)


def on_device(
    context_q, context_k, context_v, question, block_lengths, anchor_index, question_length
):
    def swap(x):
        return lax.ppermute(x, "ctx", OTHER_CORE)

    def along_y(x):
        return [x] + [lax.ppermute(x, "ctx", Y_SHIFTS[d]) for d in range(1, NY)]

    def along_z(x, d):
        return lax.ppermute(x, "ctx", Z_SHIFTS[d]), lax.ppermute(x, "ctx", Z_SHIFTS[NZ - d])

    def with_other_core(parts):
        return parts + [swap(x) for x in parts]

    columns = along_y(join(context_k, context_v, swap(context_k), swap(context_v)))
    spread_rows = repeat(question, swap(question))
    got = lax.all_to_all(spread_rows, "ctx", 0, 0, axis_index_groups=Z_GROUPS)
    columns = [columns[0], *gate(columns[1:], got)]
    piece = pick(anchor_index, columns)
    below, above = along_z(piece, 1)
    send = question_pass(block_lengths, got, columns)
    parts = lax.all_to_all(send, "ctx", 0, 0, axis_index_groups=Z_GROUPS)
    distance = (lax.axis_index("ctx") // (NY * NC) - anchor_index[0] // (NY * NC)) & (NZ - 1)
    piece = jnp.where(distance == 1, below, jnp.where(distance == NZ - 1, above, piece))
    below, above = along_z(piece, 3)
    near = (distance < 2) | (distance == NZ - 1)
    piece = jnp.where(near, piece, jnp.where(distance < 5, below, above))
    spread = combine(question_length, parts, piece)
    own = lax.all_to_all(spread, "ctx", 0, 0, axis_index_groups=CHIP_GROUPS)
    pieces = [piece, lax.ppermute(piece, "ctx", Y_SHIFTS[1])]
    mixed, key_cache, value_cache, token = encode(
        anchor_index,
        block_lengths,
        context_q,
        context_k,
        context_v,
        pieces + [swap(x) for x in pieces],
    )
    (own,) = gate([own], token)
    answer = assemble(own, swap(own))
    return mixed, key_cache, value_cache, answer


def solution(mesh):
    placed = (
        P("ctx", "heads"),
        P("ctx", "heads"),
        P("ctx", "heads"),
        P("ctx", "heads"),
        P(),
        P(),
        P(),
    )
    return jax.shard_map(
        on_device,
        mesh=mesh,
        in_specs=placed,
        out_specs=(P("ctx", "heads"), P("ctx", "heads"), P("ctx", "heads"), P(None, "heads")),
        check_vma=False,
    )
```

```python
import functools
import math

import jax
import jax.numpy as jnp
from jax import lax
from jax.experimental import pallas as pl
from jax.experimental.pallas import tpu as pltpu
from jax.sharding import PartitionSpec as P

HD = 128
SC = HD ** (-0.5)
SC2 = SC * math.log2(math.e)
NZ, NY, NC = 8, 4, 2
BLK = 256
BF = jnp.bfloat16
F32 = jnp.float32
SMEM = pl.BlockSpec(memory_space=pltpu.SMEM)
VMEM = pl.BlockSpec(memory_space=pltpu.VMEM)
SMALL = pltpu.CompilerParams(vmem_limit_bytes=4 * 1024 * 1024)
PARAMS = pltpu.CompilerParams(vmem_limit_bytes=20 * 1024 * 1024)


def index_of(z, y, c):
    return (z * NY + y) * NC + c


def permutation(move):
    return [
        (index_of(z, y, c), index_of(*move(z, y, c)))
        for z in range(NZ)
        for y in range(NY)
        for c in range(NC)
    ]


Z_GROUPS = [[index_of(z, y, c) for z in range(NZ)] for y in range(NY) for c in range(NC)]
CHIP_GROUPS = [[index_of(z, y, c) for z in range(NZ) for y in range(NY)] for c in range(NC)]
OTHER_CORE = permutation(lambda z, y, c: (z, y, 1 - c))
Y_PARTNER = permutation(lambda z, y, c: (z, y ^ 1, c))
DIAGONAL = permutation(lambda z, y, c: (z, y ^ 1, 1 - c))
Y_SHIFTS = [permutation(lambda z, y, c, d=d: (z, (y + d) % NY, c)) for d in range(NY)]
Z_SHIFTS = [permutation(lambda z, y, c, d=d: ((z + d) % NZ, y, c)) for d in range(NZ)]


def coordinates():
    place = lax.axis_index("ctx")
    return place // (NY * NC), (place // NC) % NY, place % NC


def sign_table():
    shape = (HD, HD)
    both = lax.broadcasted_iota(jnp.int32, shape, 0) & lax.broadcasted_iota(jnp.int32, shape, 1)
    both = both ^ (both >> 4)
    both = both ^ (both >> 2)
    both = both ^ (both >> 1)
    return (1 - 2 * (both & 1)).astype(F32).astype(BF)


def across(a, b):
    return lax.dot_general(a, b, (((1,), (1,)), ((), ())), preferred_element_type=F32)


def dot(a, b):
    return jnp.dot(a, b, preferred_element_type=F32)


def rotated(rows, table):
    return (dot(rows, table) * SC).astype(BF)


def halve_kernel(k_ref, v_ref, mine_ref):
    c = coordinates()[2]
    for head in range(NC):

        @pl.when(c == head)
        def _(head=head):
            lanes = slice(HD * head, HD * head + HD)
            mine_ref[0:BLK, :] = k_ref[:, lanes]
            mine_ref[BLK : 2 * BLK, :] = v_ref[:, lanes]


def halve(k, v):
    return pl.pallas_call(
        halve_kernel,
        out_shape=jax.ShapeDtypeStruct((2 * BLK, HD), BF),
        in_specs=[VMEM] * 2,
        out_specs=VMEM,
        compiler_params=SMALL,
        name="halve",
    )(k, v)


def join_kernel(mine_ref, k_ref, v_ref, early_ref, both_ref):
    c = coordinates()[2]
    both_ref[0 : 2 * BLK, :] = mine_ref[...]
    for head in range(NC):

        @pl.when(c == head)
        def _(head=head):
            lanes = slice(HD * head, HD * head + HD)
            both_ref[2 * BLK : 3 * BLK, :] = k_ref[:, lanes]
            both_ref[3 * BLK : 4 * BLK, :] = v_ref[:, lanes]


def join(mine, k_other, v_other, early):
    return pl.pallas_call(
        join_kernel,
        out_shape=jax.ShapeDtypeStruct((4 * BLK, HD), BF),
        in_specs=[VMEM] * 3 + [pl.BlockSpec(memory_space=pl.ANY)],
        out_specs=VMEM,
        compiler_params=SMALL,
        name="join",
    )(mine, k_other, v_other, early)


def repeat_kernel(own_ref, other_ref, send_ref, rows_ref):
    c = coordinates()[2]
    own, other = own_ref[...].astype(F32), other_ref[...].astype(F32)
    first, second = jnp.where(c == 0, own, other), jnp.where(c == 0, other, own)
    for at, source in enumerate((first, second)):
        for j in range(8):
            left, right = source[:, HD * j : HD * j + HD], source[:, HD * (8 + j) : HD * (9 + j)]
            rows_ref[8 * j + 4 * at : 8 * j + 4 * at + 4, :] = jnp.where(c == 0, left, right)
    rows = rows_ref[...].astype(BF)
    for i in range(NZ):
        send_ref[i] = rows


def repeat(own, other):
    return pl.pallas_call(
        repeat_kernel,
        out_shape=jax.ShapeDtypeStruct((NZ, 64, HD), BF),
        in_specs=[VMEM] * 2,
        out_specs=VMEM,
        scratch_shapes=[pltpu.VMEM((64, HD), F32)],
        compiler_params=SMALL,
        name="repeat",
    )(own, other)


def gate_kernel(*refs):
    pass


def gate(arrays, token):
    anywhere = pl.BlockSpec(memory_space=pl.ANY)
    return pl.pallas_call(
        gate_kernel,
        out_shape=[jax.ShapeDtypeStruct(x.shape, x.dtype) for x in arrays],
        in_specs=[anywhere] * (len(arrays) + 1),
        out_specs=[anywhere] * len(arrays),
        input_output_aliases={i: i for i in range(len(arrays))},
        compiler_params=pltpu.CompilerParams(vmem_limit_bytes=1024 * 1024),
        name="gate",
    )(*arrays, token)


def pick_kernel(anchor_ref, *refs):
    columns, out_ref = refs[:NY], refs[NY]
    z, y, c = coordinates()
    wanted = lax.rem(anchor_ref[0], NY * NC)
    rows = HD * lax.rem(y, 2)
    for which in range(8):
        core = c if which < NY else 1 - c
        place = NC * lax.rem(y + NY - which % NY, NY) + core

        @pl.when(place == wanted)
        def _(which=which):
            for i in range(2):
                first = pl.multiple_of(2 * BLK * (which // NY) + BLK * i + rows, HD)
                out_ref[HD * i : HD * i + HD, :] = columns[which % NY][pl.ds(first, HD), :]


def pick(anchor_index, columns):
    return pl.pallas_call(
        pick_kernel,
        out_shape=jax.ShapeDtypeStruct((BLK, HD), BF),
        in_specs=[SMEM] + [VMEM] * NY,
        out_specs=VMEM,
        compiler_params=SMALL,
        name="pick",
    )(anchor_index, *columns)


def thirds(x):
    high = x.astype(BF)
    rest = x - high.astype(F32)
    middle = rest.astype(BF)
    return high, middle, (rest - middle.astype(F32)).astype(BF)


def question_kernel(lengths_ref, got_ref, *refs):
    columns, send_ref = refs[:NY], refs[NY]
    z, y, c = coordinates()
    table = sign_table()
    lane = lax.broadcasted_iota(jnp.int32, (BLK, BLK), 1)
    ids = [index_of(z, lax.rem(y + NY - d, NY), c) for d in range(NY)]
    ids += [index_of(z, lax.rem(y + NY - d, NY), 1 - c) for d in range(NY)]
    q = rotated(got_ref[...].reshape(NZ * 64, HD), table)
    halves = [q[0:BLK], q[BLK : 2 * BLK]]
    tops, totals, sums = [None] * 2, [None] * 2, [None] * 2
    for which in range(8):
        column, first = columns[which % NY], 2 * BLK * (which // NY)
        k = rotated(column[first : first + BLK, :], table)
        v = rotated(column[first + BLK : first + 2 * BLK, :], table)
        ok = lane < lengths_ref[ids[which]]
        for i in range(2):
            part = jnp.where(ok, across(halves[i], k) * SC2, -jnp.inf)
            m = jnp.max(part, axis=1, keepdims=True)
            e = jnp.exp2(part - m)
            d = jnp.sum(e, axis=1, keepdims=True)
            n = dot(e.astype(BF), v)
            if which == 0:
                tops[i], totals[i], sums[i] = m, d, n
            else:
                new = jnp.maximum(tops[i], m)
                old_scale, scale = jnp.exp2(tops[i] - new), jnp.exp2(m - new)
                tops[i] = new
                totals[i] = totals[i] * old_scale + d * scale
                sums[i] = sums[i] * old_scale + n * scale
    lanes = lax.broadcasted_iota(jnp.int32, (HD, HD), 1)
    packed = jnp.zeros((HD, HD), F32)
    for i in range(4):
        rows = slice(HD * (i % 2), HD * (i % 2) + HD)
        packed = jnp.where(lanes == i, tops[i // 2][rows], packed)
        packed = jnp.where(lanes == 4 + i, totals[i // 2][rows], packed)
    tile = packed.T[0:8, :]
    for i in range(2):
        send_ref[4 * i : 4 * i + 4, 0:64, :] = sums[i].reshape(4, 64, HD)
    for i in range(NZ):
        send_ref[i, 64:72, :] = tile


def question_pass(lengths, got, columns):
    return pl.pallas_call(
        question_kernel,
        out_shape=jax.ShapeDtypeStruct((NZ, 72, HD), F32),
        in_specs=[SMEM] + [VMEM] * (1 + NY),
        out_specs=VMEM,
        compiler_params=PARAMS,
        cost_estimate=pl.CostEstimate(
            flops=900_000_000, bytes_accessed=2_500_000, transcendentals=1_100_000
        ),
        name="question_pass",
    )(lengths, got, *columns)


def combine_kernel(limit_ref, parts_ref, piece_ref, send_ref, columns_ref):
    z, y, c = coordinates()
    table = sign_table()
    tops = [parts_ref[s, pl.ds(64 + z // 2, 1), :] for s in range(NZ)]
    totals = [parts_ref[s, pl.ds(68 + z // 2, 1), :] for s in range(NZ)]
    square = jnp.concatenate(tops + totals + [jnp.zeros((HD - 16, HD), F32)], axis=0)
    columns_ref[...] = square.T
    columns = columns_ref[pl.ds(pl.multiple_of(z % 2 * 64, 64), 64), :]
    row = lax.broadcasted_iota(jnp.int32, (64, HD), 0)
    tops = [columns[:, s : s + 1] for s in range(NZ)]
    peak = functools.reduce(jnp.maximum, tops)
    total = jnp.zeros((64, 1), F32)
    summed = jnp.zeros((64, HD), F32)
    for s in range(NZ):
        scale = jnp.exp2(tops[s] - peak)
        total = total + scale * columns[:, NZ + s : NZ + s + 1]
        summed = summed + scale * parts_ref[s, 0:64, :]
    high, middle, low = thirds(summed / total)
    back = (dot(low, table) + dot(middle, table) + dot(high, table)) * SC
    position = (z * NY + y) * 8 + (row & 7)
    back = jnp.where(position < limit_ref[0], back, 0.0).astype(BF)
    back = back.astype(F32).reshape(8, 8, HD).astype(BF)
    for i in range(NZ * NY):
        send_ref[i] = back


def combine(limit, parts, piece):
    return pl.pallas_call(
        combine_kernel,
        out_shape=jax.ShapeDtypeStruct((NZ * NY, 8, 8, HD), BF),
        in_specs=[SMEM, VMEM, pl.BlockSpec(memory_space=pl.ANY)],
        out_specs=VMEM,
        scratch_shapes=[pltpu.VMEM((HD, HD), F32)],
        compiler_params=SMALL,
        name="combine",
    )(limit, parts, piece)


def encode_kernel(anchor_ref, lengths_ref, q_ref, k_ref, v_ref, *refs):
    pieces = refs[:4]
    mixed_ref, krot_ref, vrot_ref, token_ref, far_k_ref, far_v_ref = refs[4:]
    z, y, c = coordinates()
    place = index_of(z, y, c)
    anchor = anchor_ref[0]
    k, v = k_ref[...], v_ref[...]
    table = sign_table()
    krot_ref[...] = rotated(k, table)
    vrot_ref[...] = rotated(v, table)
    token_ref[...] = jnp.zeros_like(token_ref)
    g = pl.program_id(0)
    for core in range(2):

        @pl.when((g == c) == (core == 0))
        def _(core=core):
            for i in range(2):
                at = pl.multiple_of(HD * lax.rem(y + i, 2), HD)
                far_k_ref[pl.ds(at, HD), :] = pieces[2 * core + i][0:HD, :]
                far_v_ref[pl.ds(at, HD), :] = pieces[2 * core + i][HD : 2 * HD, :]

    far_k, far_v = far_k_ref[...], far_v_ref[...]
    far_len = jnp.where(place == anchor, 0, lengths_ref[anchor])
    own_len = lengths_ref[place]
    query = lax.broadcasted_iota(jnp.int32, (BLK, BLK), 0)
    key = lax.broadcasted_iota(jnp.int32, (BLK, BLK), 1)
    far_ok = key < far_len
    own_ok = (key <= query) & (key < own_len)
    for j in range(8):
        q = q_ref[:, HD * j : HD * j + HD]
        s_far = jnp.where(far_ok, across(q, far_k) * SC2, -jnp.inf)
        s_own = jnp.where(own_ok, across(q, k) * SC2, -jnp.inf)
        top = jnp.max(jnp.maximum(s_far, s_own), axis=1, keepdims=True)
        e_far = jnp.exp2(s_far - top)
        e_own = jnp.exp2(s_own - top)
        total = jnp.sum(e_far + e_own, axis=1, keepdims=True)
        summed = dot(e_far.astype(BF), far_v) + dot(e_own.astype(BF), v)
        mixed_ref[:, HD * j : HD * j + HD] = (summed / total).astype(BF)


def encode(anchor_index, lengths, q, k, v, pieces):
    heads = pl.BlockSpec((BLK, 8 * HD), lambda g: (0, g))
    group = pl.BlockSpec((BLK, HD), lambda g: (0, g))
    token = pl.BlockSpec((8, HD), lambda g: (0, 0))
    return pl.pallas_call(
        encode_kernel,
        grid=(2,),
        out_shape=(
            jax.ShapeDtypeStruct(q.shape, BF),
            jax.ShapeDtypeStruct(k.shape, BF),
            jax.ShapeDtypeStruct(v.shape, BF),
            jax.ShapeDtypeStruct((8, HD), F32),
        ),
        in_specs=[SMEM, SMEM, heads, group, group] + [VMEM] * 4,
        out_specs=(heads, group, group, token),
        scratch_shapes=[pltpu.VMEM((BLK, HD), BF), pltpu.VMEM((BLK, HD), BF)],
        compiler_params=PARAMS,
        cost_estimate=pl.CostEstimate(
            flops=1_100_000_000, bytes_accessed=3_500_000, transcendentals=2_100_000
        ),
        name="encode",
    )(anchor_index, lengths, q, k, v, *pieces)


def assemble_kernel(part_ref, *refs, own):
    out_ref, sems = refs[-2:]
    c = coordinates()[2]
    head = c if own else 1 - c
    copies = []
    for j in range(8):
        lanes = pl.ds(pl.multiple_of(HD * (8 * head + j), HD), HD)
        copies.append(pltpu.make_async_copy(part_ref.at[:, j], out_ref.at[:, :, lanes], sems.at[j]))
    for copy in copies:
        copy.start()
    for copy in copies:
        copy.wait()


def assemble(part, out=None):
    anywhere = pl.BlockSpec(memory_space=pl.ANY)
    return pl.pallas_call(
        functools.partial(assemble_kernel, own=out is None),
        out_shape=jax.ShapeDtypeStruct((32, 8, 2048), BF),
        in_specs=[anywhere] * (1 if out is None else 2),
        out_specs=anywhere,
        scratch_shapes=[pltpu.SemaphoreType.DMA((8,))],
        input_output_aliases={} if out is None else {1: 0},
        compiler_params=SMALL,
        name="assemble",
    )(part, *([] if out is None else [out]))


def on_device(
    context_q, context_k, context_v, question, block_lengths, anchor_index, question_length
):
    def swap(x):
        return lax.ppermute(x, "ctx", OTHER_CORE)

    def along_y(x):
        return [x] + [lax.ppermute(x, "ctx", Y_SHIFTS[d]) for d in range(1, NY)]

    def along_z(x, d):
        return lax.ppermute(x, "ctx", Z_SHIFTS[d]), lax.ppermute(x, "ctx", Z_SHIFTS[NZ - d])

    def with_other_core(parts):
        return parts + [swap(x) for x in parts]

    mine = halve(context_k, context_v)
    other_question = swap(question)
    columns = along_y(join(mine, swap(context_k), swap(context_v), other_question))
    spread_rows = repeat(question, other_question)
    got = lax.all_to_all(spread_rows, "ctx", 0, 0, axis_index_groups=Z_GROUPS)
    columns = [columns[0], *gate(columns[1:], got)]
    piece = pick(anchor_index, columns)
    below, above = along_z(piece, 1)
    send = question_pass(block_lengths, got, columns)
    parts = lax.all_to_all(send, "ctx", 0, 0, axis_index_groups=Z_GROUPS)
    distance = (lax.axis_index("ctx") // (NY * NC) - anchor_index[0] // (NY * NC)) & (NZ - 1)
    piece = jnp.where(distance == 1, below, jnp.where(distance == NZ - 1, above, piece))
    below, above = along_z(piece, 3)
    near = (distance < 2) | (distance == NZ - 1)
    piece = jnp.where(near, piece, jnp.where(distance < 5, below, above))
    spread = combine(question_length, parts, piece)
    own = lax.all_to_all(spread, "ctx", 0, 0, axis_index_groups=CHIP_GROUPS)
    pieces = [piece, lax.ppermute(piece, "ctx", Y_PARTNER)]
    pieces = pieces + [swap(piece), lax.ppermute(piece, "ctx", DIAGONAL)]
    mixed, key_cache, value_cache, token = encode(
        anchor_index,
        block_lengths,
        context_q,
        context_k,
        context_v,
        pieces,
    )
    (own,) = gate([own], token)
    answer = assemble(swap(own), assemble(own)).reshape(256, 2048)
    return mixed, key_cache, value_cache, answer


def solution(mesh):
    placed = (
        P("ctx", "heads"),
        P("ctx", "heads"),
        P("ctx", "heads"),
        P("ctx", "heads"),
        P(),
        P(),
        P(),
    )
    return jax.shard_map(
        on_device,
        mesh=mesh,
        in_specs=placed,
        out_specs=(P("ctx", "heads"), P("ctx", "heads"), P("ctx", "heads"), P(None, "heads")),
        check_vma=False,
    )
```

```python
import functools
import math

import jax
import jax.numpy as jnp
from jax import lax
from jax.experimental import pallas as pl
from jax.experimental.pallas import tpu as pltpu
from jax.sharding import PartitionSpec as P

HD = 128
SC = HD ** (-0.5)
SC2 = SC * math.log2(math.e)
NZ, NY, NC = 8, 4, 2
BLK = 256
BF = jnp.bfloat16
F32 = jnp.float32
SMEM = pl.BlockSpec(memory_space=pltpu.SMEM)
VMEM = pl.BlockSpec(memory_space=pltpu.VMEM)
SMALL = pltpu.CompilerParams(vmem_limit_bytes=4 * 1024 * 1024)
PARAMS = pltpu.CompilerParams(vmem_limit_bytes=20 * 1024 * 1024)


def index_of(z, y, c):
    return (z * NY + y) * NC + c


def permutation(move):
    return [
        (index_of(z, y, c), index_of(*move(z, y, c)))
        for z in range(NZ)
        for y in range(NY)
        for c in range(NC)
    ]


Z_GROUPS = [[index_of(z, y, c) for z in range(NZ)] for y in range(NY) for c in range(NC)]
CHIP_GROUPS = [[index_of(z, y, c) for z in range(NZ) for y in range(NY)] for c in range(NC)]
OTHER_CORE = permutation(lambda z, y, c: (z, y, 1 - c))
Y_PARTNER = permutation(lambda z, y, c: (z, y ^ 1, c))
DIAGONAL = permutation(lambda z, y, c: (z, y ^ 1, 1 - c))
Y_MOVES = [permutation(lambda z, y, c, d=d: (z, y ^ d, c)) for d in range(NY)]
Z_SHIFTS = [permutation(lambda z, y, c, d=d: ((z + d) % NZ, y, c)) for d in range(NZ)]


def coordinates():
    place = lax.axis_index("ctx")
    return place // (NY * NC), (place // NC) % NY, place % NC


def sign_table():
    shape = (HD, HD)
    both = lax.broadcasted_iota(jnp.int32, shape, 0) & lax.broadcasted_iota(jnp.int32, shape, 1)
    both = both ^ (both >> 4)
    both = both ^ (both >> 2)
    both = both ^ (both >> 1)
    return (1 - 2 * (both & 1)).astype(F32).astype(BF)


def across(a, b):
    return lax.dot_general(a, b, (((1,), (1,)), ((), ())), preferred_element_type=F32)


def dot(a, b):
    return jnp.dot(a, b, preferred_element_type=F32)


def rotated(rows, table):
    return (dot(rows, table) * SC).astype(BF)


def join_kernel(mine_ref, k_ref, v_ref, early_ref, both_ref):
    c = coordinates()[2]
    both_ref[0 : 2 * BLK, :] = mine_ref[...]
    for head in range(NC):

        @pl.when(c == head)
        def _(head=head):
            lanes = slice(HD * head, HD * head + HD)
            both_ref[2 * BLK : 3 * BLK, :] = k_ref[:, lanes]
            both_ref[3 * BLK : 4 * BLK, :] = v_ref[:, lanes]


def join(mine, k_other, v_other, early):
    return pl.pallas_call(
        join_kernel,
        out_shape=jax.ShapeDtypeStruct((4 * BLK, HD), BF),
        in_specs=[VMEM] * 3 + [pl.BlockSpec(memory_space=pl.ANY)],
        out_specs=VMEM,
        compiler_params=SMALL,
        name="join",
    )(mine, k_other, v_other, early)


def repeat_kernel(own_ref, other_ref, send_ref, rows_ref):
    c = coordinates()[2]
    own, other = own_ref[...].astype(F32), other_ref[...].astype(F32)
    first, second = jnp.where(c == 0, own, other), jnp.where(c == 0, other, own)
    for at, source in enumerate((first, second)):
        for j in range(8):
            left, right = source[:, HD * j : HD * j + HD], source[:, HD * (8 + j) : HD * (9 + j)]
            rows_ref[8 * j + 4 * at : 8 * j + 4 * at + 4, :] = jnp.where(c == 0, left, right)
    rows = rows_ref[...].astype(BF)
    for i in range(NZ):
        send_ref[i] = rows


def repeat(own, other):
    return pl.pallas_call(
        repeat_kernel,
        out_shape=jax.ShapeDtypeStruct((NZ, 64, HD), BF),
        in_specs=[VMEM] * 2,
        out_specs=VMEM,
        scratch_shapes=[pltpu.VMEM((64, HD), F32)],
        compiler_params=SMALL,
        name="repeat",
    )(own, other)


def gate_kernel(*refs):
    pass


def gate(arrays, token):
    anywhere = pl.BlockSpec(memory_space=pl.ANY)
    return pl.pallas_call(
        gate_kernel,
        out_shape=[jax.ShapeDtypeStruct(x.shape, x.dtype) for x in arrays],
        in_specs=[anywhere] * (len(arrays) + 1),
        out_specs=[anywhere] * len(arrays),
        input_output_aliases={i: i for i in range(len(arrays))},
        compiler_params=pltpu.CompilerParams(vmem_limit_bytes=1024 * 1024),
        name="gate",
    )(*arrays, token)


def pick_kernel(anchor_ref, *refs):
    columns, out_ref = refs[:NY], refs[NY]
    z, y, c = coordinates()
    wanted = lax.rem(anchor_ref[0], NY * NC)
    rows = HD * lax.rem(y, 2)
    for which in range(8):
        core = c if which < NY else 1 - c
        place = NC * (y ^ which % NY) + core

        @pl.when(place == wanted)
        def _(which=which):
            for i in range(2):
                first = pl.multiple_of(2 * BLK * (which // NY) + BLK * i + rows, HD)
                out_ref[HD * i : HD * i + HD, :] = columns[which % NY][pl.ds(first, HD), :]


def pick(anchor_index, columns):
    return pl.pallas_call(
        pick_kernel,
        out_shape=jax.ShapeDtypeStruct((BLK, HD), BF),
        in_specs=[SMEM] + [VMEM] * NY,
        out_specs=VMEM,
        compiler_params=SMALL,
        name="pick",
    )(anchor_index, *columns)


def thirds(x):
    high = x.astype(BF)
    rest = x - high.astype(F32)
    middle = rest.astype(BF)
    return high, middle, (rest - middle.astype(F32)).astype(BF)


def question_kernel(lengths_ref, got_ref, *refs):
    columns, send_ref = refs[:NY], refs[NY]
    z, y, c = coordinates()
    table = sign_table()
    lane = lax.broadcasted_iota(jnp.int32, (BLK, BLK), 1)
    ids = [index_of(z, y ^ d, c) for d in range(NY)]
    ids += [index_of(z, y ^ d, 1 - c) for d in range(NY)]
    q = rotated(got_ref[...].reshape(NZ * 64, HD), table)
    turned = [rotated(column[...], table) for column in columns]
    tops, totals, sums = [], [], []
    for i in range(2):
        chunk = q[BLK * i : BLK * i + BLK]
        top = total = summed = None
        for which in range(8):
            column, first = turned[which % NY], 2 * BLK * (which // NY)
            k, v = column[first : first + BLK], column[first + BLK : first + 2 * BLK]
            part = jnp.where(lane < lengths_ref[ids[which]], across(chunk, k) * SC2, -jnp.inf)
            m = jnp.max(part, axis=1, keepdims=True)
            e = jnp.exp2(part - m)
            d = jnp.sum(e, axis=1, keepdims=True)
            n = dot(e.astype(BF), v)
            if which == 0:
                top, total, summed = m, d, n
            else:
                new = jnp.maximum(top, m)
                old_scale, scale = jnp.exp2(top - new), jnp.exp2(m - new)
                top = new
                total = total * old_scale + d * scale
                summed = summed * old_scale + n * scale
        tops.append(top)
        totals.append(total)
        sums.append(summed)
    lanes = lax.broadcasted_iota(jnp.int32, (HD, HD), 1)
    packed = jnp.zeros((HD, HD), F32)
    for i in range(4):
        rows = slice(HD * (i % 2), HD * (i % 2) + HD)
        packed = jnp.where(lanes == i, tops[i // 2][rows], packed)
        packed = jnp.where(lanes == 4 + i, totals[i // 2][rows], packed)
    tile = packed.T[0:8, :]
    for i in range(2):
        send_ref[4 * i : 4 * i + 4, 0:64, :] = sums[i].reshape(4, 64, HD)
    for i in range(NZ):
        send_ref[i, 64:72, :] = tile


def question_pass(lengths, got, columns):
    return pl.pallas_call(
        question_kernel,
        out_shape=jax.ShapeDtypeStruct((NZ, 72, HD), F32),
        in_specs=[SMEM] + [VMEM] * (1 + NY),
        out_specs=VMEM,
        compiler_params=PARAMS,
        cost_estimate=pl.CostEstimate(
            flops=900_000_000, bytes_accessed=2_500_000, transcendentals=1_100_000
        ),
        name="question_pass",
    )(lengths, got, *columns)


def combine_kernel(limit_ref, parts_ref, piece_ref, send_ref, columns_ref):
    z, y, c = coordinates()
    table = sign_table()
    tops = [parts_ref[s, pl.ds(64 + z // 2, 1), :] for s in range(NZ)]
    totals = [parts_ref[s, pl.ds(68 + z // 2, 1), :] for s in range(NZ)]
    tops, totals = jnp.concatenate(tops, axis=0), jnp.concatenate(totals, axis=0)
    weights = jnp.exp2(tops - jnp.max(tops, axis=0, keepdims=True))
    weights = weights / jnp.sum(weights * totals, axis=0, keepdims=True)
    square = jnp.concatenate([weights, jnp.zeros((HD - NZ, HD), F32)], axis=0)
    columns_ref[...] = square.T
    columns = columns_ref[pl.ds(pl.multiple_of(z % 2 * 64, 64), 64), :]
    row = lax.broadcasted_iota(jnp.int32, (64, HD), 0)
    result = jnp.zeros((64, HD), F32)
    for s in range(NZ):
        result = result + columns[:, s : s + 1] * parts_ref[s, 0:64, :]
    high, middle, low = thirds(result)
    back = (dot(low, table) + dot(middle, table) + dot(high, table)) * SC
    position = (z * NY + y) * 8 + (row & 7)
    back = jnp.where(position < limit_ref[0], back, 0.0).astype(BF)
    back = back.astype(F32).reshape(8, 8, HD).astype(BF)
    for i in range(NZ * NY):
        send_ref[i] = back


def combine(limit, parts, piece):
    return pl.pallas_call(
        combine_kernel,
        out_shape=jax.ShapeDtypeStruct((NZ * NY, 8, 8, HD), BF),
        in_specs=[SMEM, VMEM, pl.BlockSpec(memory_space=pl.ANY)],
        out_specs=VMEM,
        scratch_shapes=[pltpu.VMEM((HD, HD), F32)],
        compiler_params=SMALL,
        name="combine",
    )(limit, parts, piece)


def encode_kernel(anchor_ref, lengths_ref, q_ref, k_ref, v_ref, *refs):
    pieces = refs[:4]
    mixed_ref, krot_ref, vrot_ref, token_ref, far_k_ref, far_v_ref = refs[4:]
    z, y, c = coordinates()
    place = index_of(z, y, c)
    anchor = anchor_ref[0]
    k, v = k_ref[...], v_ref[...]
    table = sign_table()
    krot_ref[...] = rotated(k, table)
    vrot_ref[...] = rotated(v, table)
    token_ref[...] = jnp.zeros_like(token_ref)
    g = pl.program_id(0)
    for core in range(2):

        @pl.when((g == c) == (core == 0))
        def _(core=core):
            for i in range(2):
                at = pl.multiple_of(HD * lax.rem(y + i, 2), HD)
                far_k_ref[pl.ds(at, HD), :] = pieces[2 * core + i][0:HD, :]
                far_v_ref[pl.ds(at, HD), :] = pieces[2 * core + i][HD : 2 * HD, :]

    far_k, far_v = far_k_ref[...], far_v_ref[...]
    far_len = jnp.where(place == anchor, 0, lengths_ref[anchor])
    own_len = lengths_ref[place]
    query = lax.broadcasted_iota(jnp.int32, (BLK, BLK), 0)
    key = lax.broadcasted_iota(jnp.int32, (BLK, BLK), 1)
    far_ok = key < far_len
    own_ok = (key <= query) & (key < own_len)
    for j in range(8):
        q = q_ref[:, HD * j : HD * j + HD]
        s_far = jnp.where(far_ok, across(q, far_k) * SC2, -jnp.inf)
        s_own = jnp.where(own_ok, across(q, k) * SC2, -jnp.inf)
        top = jnp.max(jnp.maximum(s_far, s_own), axis=1, keepdims=True)
        e_far = jnp.exp2(s_far - top)
        e_own = jnp.exp2(s_own - top)
        total = jnp.sum(e_far + e_own, axis=1, keepdims=True)
        summed = dot(e_far.astype(BF), far_v) + dot(e_own.astype(BF), v)
        mixed_ref[:, HD * j : HD * j + HD] = (summed / total).astype(BF)


def encode(anchor_index, lengths, q, k, v, pieces):
    heads = pl.BlockSpec((BLK, 8 * HD), lambda g: (0, g))
    group = pl.BlockSpec((BLK, HD), lambda g: (0, g))
    token = pl.BlockSpec((8, HD), lambda g: (0, 0))
    return pl.pallas_call(
        encode_kernel,
        grid=(2,),
        out_shape=(
            jax.ShapeDtypeStruct(q.shape, BF),
            jax.ShapeDtypeStruct(k.shape, BF),
            jax.ShapeDtypeStruct(v.shape, BF),
            jax.ShapeDtypeStruct((8, HD), F32),
        ),
        in_specs=[SMEM, SMEM, heads, group, group] + [VMEM] * 4,
        out_specs=(heads, group, group, token),
        scratch_shapes=[pltpu.VMEM((BLK, HD), BF), pltpu.VMEM((BLK, HD), BF)],
        compiler_params=PARAMS,
        cost_estimate=pl.CostEstimate(
            flops=1_100_000_000, bytes_accessed=3_500_000, transcendentals=2_100_000
        ),
        name="encode",
    )(anchor_index, lengths, q, k, v, *pieces)


def assemble_kernel(part_ref, *refs, own):
    out_ref, sems = refs[-2:]
    c = coordinates()[2]
    head = c if own else 1 - c
    copies = []
    for j in range(8):
        lanes = pl.ds(pl.multiple_of(HD * (8 * head + j), HD), HD)
        copies.append(pltpu.make_async_copy(part_ref.at[:, j], out_ref.at[:, :, lanes], sems.at[j]))
    for copy in copies:
        copy.start()
    for copy in copies:
        copy.wait()


def assemble(part, out=None):
    anywhere = pl.BlockSpec(memory_space=pl.ANY)
    return pl.pallas_call(
        functools.partial(assemble_kernel, own=out is None),
        out_shape=jax.ShapeDtypeStruct((32, 8, 2048), BF),
        in_specs=[anywhere] * (1 if out is None else 2),
        out_specs=anywhere,
        scratch_shapes=[pltpu.SemaphoreType.DMA((8,))],
        input_output_aliases={} if out is None else {1: 0},
        compiler_params=SMALL,
        name="assemble",
    )(part, *([] if out is None else [out]))


def on_device(
    context_q, context_k, context_v, question, block_lengths, anchor_index, question_length
):
    def swap(x):
        return lax.ppermute(x, "ctx", OTHER_CORE)

    def along_y(x):
        return [x] + [lax.ppermute(x, "ctx", Y_MOVES[d]) for d in range(1, NY)]

    def along_z(x, d):
        return lax.ppermute(x, "ctx", Z_SHIFTS[d]), lax.ppermute(x, "ctx", Z_SHIFTS[NZ - d])

    def with_other_core(parts):
        return parts + [swap(x) for x in parts]

    first_lane = lax.axis_index("ctx") % NC * HD
    halves = [lax.dynamic_slice_in_dim(x, first_lane, HD, 1) for x in (context_k, context_v)]
    mine = jnp.concatenate(halves, axis=0)
    other_question = swap(question)
    columns = along_y(join(mine, swap(context_k), swap(context_v), other_question))
    spread_rows = repeat(question, other_question)
    got = lax.all_to_all(spread_rows, "ctx", 0, 0, axis_index_groups=Z_GROUPS)
    columns = [columns[0], *gate(columns[1:], got)]
    piece = pick(anchor_index, columns)
    below, above = along_z(piece, 1)
    send = question_pass(block_lengths, got, columns)
    parts = lax.all_to_all(send, "ctx", 0, 0, axis_index_groups=Z_GROUPS)
    distance = (lax.axis_index("ctx") // (NY * NC) - anchor_index[0] // (NY * NC)) & (NZ - 1)
    piece = jnp.where(distance == 1, below, jnp.where(distance == NZ - 1, above, piece))
    below, above = along_z(piece, 3)
    near = (distance < 2) | (distance == NZ - 1)
    piece = jnp.where(near, piece, jnp.where(distance < 5, below, above))
    spread = combine(question_length, parts, piece)
    own = lax.all_to_all(spread, "ctx", 0, 0, axis_index_groups=CHIP_GROUPS)
    pieces = [piece, lax.ppermute(piece, "ctx", Y_PARTNER)]
    pieces = pieces + [swap(piece), lax.ppermute(piece, "ctx", DIAGONAL)]
    mixed, key_cache, value_cache, token = encode(
        anchor_index,
        block_lengths,
        context_q,
        context_k,
        context_v,
        pieces,
    )
    (own,) = gate([own], token)
    answer = assemble(swap(own), assemble(own)).reshape(256, 2048)
    return mixed, key_cache, value_cache, answer


def solution(mesh):
    placed = (
        P("ctx", "heads"),
        P("ctx", "heads"),
        P("ctx", "heads"),
        P("ctx", "heads"),
        P(),
        P(),
        P(),
    )
    return jax.shard_map(
        on_device,
        mesh=mesh,
        in_specs=placed,
        out_specs=(P("ctx", "heads"), P("ctx", "heads"), P("ctx", "heads"), P(None, "heads")),
        check_vma=False,
    )
```

```python
import functools
import math

import jax
import jax.numpy as jnp
from jax import lax
from jax.experimental import pallas as pl
from jax.experimental.pallas import tpu as pltpu
from jax.sharding import PartitionSpec as P

HD = 128
SC = HD ** (-0.5)
SC2 = SC * math.log2(math.e)
NZ, NY, NC = 8, 4, 2
BLK = 256
BF = jnp.bfloat16
F32 = jnp.float32
SMEM = pl.BlockSpec(memory_space=pltpu.SMEM)
VMEM = pl.BlockSpec(memory_space=pltpu.VMEM)
SMALL = pltpu.CompilerParams(vmem_limit_bytes=4 * 1024 * 1024)
PARAMS = pltpu.CompilerParams(vmem_limit_bytes=20 * 1024 * 1024)


def index_of(z, y, c):
    return (z * NY + y) * NC + c


def permutation(move):
    return [
        (index_of(z, y, c), index_of(*move(z, y, c)))
        for z in range(NZ)
        for y in range(NY)
        for c in range(NC)
    ]


Z_ORDER = (0, 2, 4, 6, 1, 3, 5, 7)
Z_GROUPS = [[index_of(z, y, c) for z in Z_ORDER] for y in range(NY) for c in range(NC)]
CHIP_GROUPS = [[index_of(z, y, c) for y in range(NY) for z in Z_ORDER] for c in range(NC)]
OTHER_CORE = permutation(lambda z, y, c: (z, y, 1 - c))
Y_PARTNER = permutation(lambda z, y, c: (z, y ^ 1, c))
DIAGONAL = permutation(lambda z, y, c: (z, y ^ 1, 1 - c))
Y_MOVES = [permutation(lambda z, y, c, d=d: (z, y ^ d, c)) for d in range(NY)]
Z_SHIFTS = [permutation(lambda z, y, c, d=d: ((z + d) % NZ, y, c)) for d in range(NZ)]


def coordinates():
    place = lax.axis_index("ctx")
    return place // (NY * NC), (place // NC) % NY, place % NC


def sign_table():
    shape = (HD, HD)
    both = lax.broadcasted_iota(jnp.int32, shape, 0) & lax.broadcasted_iota(jnp.int32, shape, 1)
    both = both ^ (both >> 4)
    both = both ^ (both >> 2)
    both = both ^ (both >> 1)
    return (1 - 2 * (both & 1)).astype(F32).astype(BF)


def across(a, b):
    return lax.dot_general(a, b, (((1,), (1,)), ((), ())), preferred_element_type=F32)


def dot(a, b):
    return jnp.dot(a, b, preferred_element_type=F32)


def rotated(rows, table):
    return (dot(rows, table) * SC).astype(BF)


def join_kernel(mine_ref, k_ref, v_ref, early_ref, both_ref):
    c = coordinates()[2]
    both_ref[0 : 2 * BLK, :] = mine_ref[...]
    for head in range(NC):

        @pl.when(c == head)
        def _(head=head):
            lanes = slice(HD * head, HD * head + HD)
            both_ref[2 * BLK : 3 * BLK, :] = k_ref[:, lanes]
            both_ref[3 * BLK : 4 * BLK, :] = v_ref[:, lanes]


def join(mine, k_other, v_other, early):
    return pl.pallas_call(
        join_kernel,
        out_shape=jax.ShapeDtypeStruct((4 * BLK, HD), BF),
        in_specs=[VMEM] * 3 + [pl.BlockSpec(memory_space=pl.ANY)],
        out_specs=VMEM,
        compiler_params=SMALL,
        name="join",
    )(mine, k_other, v_other, early)


def repeat_kernel(own_ref, other_ref, send_ref, rows_ref):
    c = coordinates()[2]
    own, other = own_ref[...].astype(F32), other_ref[...].astype(F32)
    first, second = jnp.where(c == 0, own, other), jnp.where(c == 0, other, own)
    for at, source in enumerate((first, second)):
        for j in range(8):
            left, right = source[:, HD * j : HD * j + HD], source[:, HD * (8 + j) : HD * (9 + j)]
            rows_ref[8 * j + 4 * at : 8 * j + 4 * at + 4, :] = jnp.where(c == 0, left, right)
    rows = rows_ref[...].astype(BF)
    for i in range(NZ):
        send_ref[i] = rows


def repeat(own, other):
    return pl.pallas_call(
        repeat_kernel,
        out_shape=jax.ShapeDtypeStruct((NZ, 64, HD), BF),
        in_specs=[VMEM] * 2,
        out_specs=VMEM,
        scratch_shapes=[pltpu.VMEM((64, HD), F32)],
        compiler_params=SMALL,
        name="repeat",
    )(own, other)


def gate_kernel(*refs):
    pass


def gate(arrays, token):
    anywhere = pl.BlockSpec(memory_space=pl.ANY)
    return pl.pallas_call(
        gate_kernel,
        out_shape=[jax.ShapeDtypeStruct(x.shape, x.dtype) for x in arrays],
        in_specs=[anywhere] * (len(arrays) + 1),
        out_specs=[anywhere] * len(arrays),
        input_output_aliases={i: i for i in range(len(arrays))},
        compiler_params=pltpu.CompilerParams(vmem_limit_bytes=1024 * 1024),
        name="gate",
    )(*arrays, token)


def pick_kernel(anchor_ref, *refs):
    columns, out_ref = refs[:NY], refs[NY]
    z, y, c = coordinates()
    wanted = lax.rem(anchor_ref[0], NY * NC)
    rows = HD * lax.rem(y, 2)
    for which in range(8):
        core = c if which < NY else 1 - c
        place = NC * (y ^ which % NY) + core

        @pl.when(place == wanted)
        def _(which=which):
            for i in range(2):
                first = pl.multiple_of(2 * BLK * (which // NY) + BLK * i + rows, HD)
                out_ref[HD * i : HD * i + HD, :] = columns[which % NY][pl.ds(first, HD), :]


def pick(anchor_index, columns):
    return pl.pallas_call(
        pick_kernel,
        out_shape=jax.ShapeDtypeStruct((BLK, HD), BF),
        in_specs=[SMEM] + [VMEM] * NY,
        out_specs=VMEM,
        compiler_params=SMALL,
        name="pick",
    )(anchor_index, *columns)


def thirds(x):
    high = x.astype(BF)
    rest = x - high.astype(F32)
    middle = rest.astype(BF)
    return high, middle, (rest - middle.astype(F32)).astype(BF)


def question_kernel(lengths_ref, got_ref, *refs):
    columns, send_ref = refs[:NY], refs[NY]
    z, y, c = coordinates()
    table = sign_table()
    lane = lax.broadcasted_iota(jnp.int32, (BLK, BLK), 1)
    ids = [index_of(z, y ^ d, c) for d in range(NY)]
    ids += [index_of(z, y ^ d, 1 - c) for d in range(NY)]
    q = rotated(got_ref[...].reshape(NZ * 64, HD), table)
    turned = [rotated(column[...], table) for column in columns]
    tops, totals, sums = [], [], []
    for i in range(2):
        chunk = q[BLK * i : BLK * i + BLK]
        top = total = summed = None
        for which in range(8):
            column, first = turned[which % NY], 2 * BLK * (which // NY)
            k, v = column[first : first + BLK], column[first + BLK : first + 2 * BLK]
            part = jnp.where(lane < lengths_ref[ids[which]], across(chunk, k) * SC2, -jnp.inf)
            m = jnp.max(part, axis=1, keepdims=True)
            e = jnp.exp2(part - m)
            d = jnp.sum(e, axis=1, keepdims=True)
            n = dot(e.astype(BF), v)
            if which == 0:
                top, total, summed = m, d, n
            else:
                new = jnp.maximum(top, m)
                old_scale, scale = jnp.exp2(top - new), jnp.exp2(m - new)
                top = new
                total = total * old_scale + d * scale
                summed = summed * old_scale + n * scale
        tops.append(top)
        totals.append(total)
        sums.append(summed)
    lanes = lax.broadcasted_iota(jnp.int32, (HD, HD), 1)
    packed = jnp.zeros((HD, HD), F32)
    for i in range(4):
        rows = slice(HD * (i % 2), HD * (i % 2) + HD)
        packed = jnp.where(lanes == i, tops[i // 2][rows], packed)
        packed = jnp.where(lanes == 4 + i, totals[i // 2][rows], packed)
    tile = packed.T[0:8, :]
    for i in range(2):
        send_ref[4 * i : 4 * i + 4, 0:64, :] = sums[i].reshape(4, 64, HD)
    for i in range(NZ):
        send_ref[i, 64:72, :] = tile


def question_pass(lengths, got, columns):
    return pl.pallas_call(
        question_kernel,
        out_shape=jax.ShapeDtypeStruct((NZ, 72, HD), F32),
        in_specs=[SMEM] + [VMEM] * (1 + NY),
        out_specs=VMEM,
        compiler_params=PARAMS,
        cost_estimate=pl.CostEstimate(
            flops=900_000_000, bytes_accessed=2_500_000, transcendentals=1_100_000
        ),
        name="question_pass",
    )(lengths, got, *columns)


def combine_kernel(limit_ref, parts_ref, piece_ref, send_ref, columns_ref):
    z, y, c = coordinates()
    table = sign_table()
    rank = z % 2 * 4 + z // 2
    tops = [parts_ref[s, pl.ds(64 + rank // 2, 1), :] for s in range(NZ)]
    totals = [parts_ref[s, pl.ds(68 + rank // 2, 1), :] for s in range(NZ)]
    tops, totals = jnp.concatenate(tops, axis=0), jnp.concatenate(totals, axis=0)
    weights = jnp.exp2(tops - jnp.max(tops, axis=0, keepdims=True))
    weights = weights / jnp.sum(weights * totals, axis=0, keepdims=True)
    square = jnp.concatenate([weights, jnp.zeros((HD - NZ, HD), F32)], axis=0)
    columns_ref[...] = square.T
    columns = columns_ref[pl.ds(pl.multiple_of(rank % 2 * 64, 64), 64), :]
    row = lax.broadcasted_iota(jnp.int32, (64, HD), 0)
    result = jnp.zeros((64, HD), F32)
    for s in range(NZ):
        result = result + columns[:, s : s + 1] * parts_ref[s, 0:64, :]
    high, middle, low = thirds(result)
    back = (dot(low, table) + dot(middle, table) + dot(high, table)) * SC
    position = (z * NY + y) * 8 + (row & 7)
    back = jnp.where(position < limit_ref[0], back, 0.0)
    back = jnp.concatenate([back[8 * j : 8 * j + 8] for j in range(8)], axis=1).astype(BF)
    for i in range(NZ * NY):
        send_ref[i] = back


def combine(limit, parts, piece):
    return pl.pallas_call(
        combine_kernel,
        out_shape=jax.ShapeDtypeStruct((NZ * NY, 8, 1024), BF),
        in_specs=[SMEM, VMEM, pl.BlockSpec(memory_space=pl.ANY)],
        out_specs=VMEM,
        scratch_shapes=[pltpu.VMEM((HD, HD), F32)],
        compiler_params=SMALL,
        name="combine",
    )(limit, parts, piece)


def encode_kernel(anchor_ref, lengths_ref, q_ref, k_ref, v_ref, *refs):
    pieces = refs[:4]
    mixed_ref, krot_ref, vrot_ref, token_ref, far_k_ref, far_v_ref = refs[4:]
    z, y, c = coordinates()
    place = index_of(z, y, c)
    anchor = anchor_ref[0]
    k, v = k_ref[...], v_ref[...]
    table = sign_table()
    krot_ref[...] = rotated(k, table)
    vrot_ref[...] = rotated(v, table)
    token_ref[...] = jnp.zeros_like(token_ref)
    g = pl.program_id(0)
    for core in range(2):

        @pl.when((g == c) == (core == 0))
        def _(core=core):
            for i in range(2):
                at = pl.multiple_of(HD * lax.rem(y + i, 2), HD)
                far_k_ref[pl.ds(at, HD), :] = pieces[2 * core + i][0:HD, :]
                far_v_ref[pl.ds(at, HD), :] = pieces[2 * core + i][HD : 2 * HD, :]

    far_k, far_v = far_k_ref[...], far_v_ref[...]
    far_len = jnp.where(place == anchor, 0, lengths_ref[anchor])
    own_len = lengths_ref[place]
    query = lax.broadcasted_iota(jnp.int32, (BLK, BLK), 0)
    key = lax.broadcasted_iota(jnp.int32, (BLK, BLK), 1)
    far_ok = key < far_len
    own_ok = (key <= query) & (key < own_len)
    for j in range(8):
        q = q_ref[:, HD * j : HD * j + HD]
        s_far = jnp.where(far_ok, across(q, far_k) * SC2, -jnp.inf)
        s_own = jnp.where(own_ok, across(q, k) * SC2, -jnp.inf)
        top = jnp.max(jnp.maximum(s_far, s_own), axis=1, keepdims=True)
        e_far = jnp.exp2(s_far - top)
        e_own = jnp.exp2(s_own - top)
        total = jnp.sum(e_far + e_own, axis=1, keepdims=True)
        summed = dot(e_far.astype(BF), far_v) + dot(e_own.astype(BF), v)
        mixed_ref[:, HD * j : HD * j + HD] = (summed / total).astype(BF)


def encode(anchor_index, lengths, q, k, v, pieces):
    heads = pl.BlockSpec((BLK, 8 * HD), lambda g: (0, g))
    group = pl.BlockSpec((BLK, HD), lambda g: (0, g))
    token = pl.BlockSpec((8, HD), lambda g: (0, 0))
    return pl.pallas_call(
        encode_kernel,
        grid=(2,),
        out_shape=(
            jax.ShapeDtypeStruct(q.shape, BF),
            jax.ShapeDtypeStruct(k.shape, BF),
            jax.ShapeDtypeStruct(v.shape, BF),
            jax.ShapeDtypeStruct((8, HD), F32),
        ),
        in_specs=[SMEM, SMEM, heads, group, group] + [VMEM] * 4,
        out_specs=(heads, group, group, token),
        scratch_shapes=[pltpu.VMEM((BLK, HD), BF), pltpu.VMEM((BLK, HD), BF)],
        compiler_params=PARAMS,
        cost_estimate=pl.CostEstimate(
            flops=1_100_000_000, bytes_accessed=3_500_000, transcendentals=2_100_000
        ),
        name="encode",
    )(anchor_index, lengths, q, k, v, *pieces)


def assemble_kernel(part_ref, *refs, own):
    out_ref, sems = refs[-2:]
    c = coordinates()[2]
    lanes = pl.ds(pl.multiple_of(1024 * (c if own else 1 - c), 1024), 1024)
    copies = []
    for y in range(NY):
        for odd in range(2):
            source = part_ref.at[pl.ds(NZ * y + 4 * odd, 4)]
            target = out_ref.at[:, odd, y, :, lanes]
            copies.append(pltpu.make_async_copy(source, target, sems.at[y, odd]))
    for copy in copies:
        copy.start()
    for copy in copies:
        copy.wait()


def assemble(part, out=None):
    anywhere = pl.BlockSpec(memory_space=pl.ANY)
    return pl.pallas_call(
        functools.partial(assemble_kernel, own=out is None),
        out_shape=jax.ShapeDtypeStruct((NZ // 2, 2, NY, 8, 2048), BF),
        in_specs=[anywhere] * (1 if out is None else 2),
        out_specs=anywhere,
        scratch_shapes=[pltpu.SemaphoreType.DMA((NY, 2))],
        input_output_aliases={} if out is None else {1: 0},
        compiler_params=SMALL,
        name="assemble",
    )(part, *([] if out is None else [out]))


def on_device(
    context_q, context_k, context_v, question, block_lengths, anchor_index, question_length
):
    def swap(x):
        return lax.ppermute(x, "ctx", OTHER_CORE)

    def along_y(x):
        return [x] + [lax.ppermute(x, "ctx", Y_MOVES[d]) for d in range(1, NY)]

    def along_z(x, d):
        return lax.ppermute(x, "ctx", Z_SHIFTS[d]), lax.ppermute(x, "ctx", Z_SHIFTS[NZ - d])

    def with_other_core(parts):
        return parts + [swap(x) for x in parts]

    first_lane = lax.axis_index("ctx") % NC * HD
    halves = [lax.dynamic_slice_in_dim(x, first_lane, HD, 1) for x in (context_k, context_v)]
    mine = jnp.concatenate(halves, axis=0)
    other_question = swap(question)
    columns = along_y(join(mine, swap(context_k), swap(context_v), other_question))
    spread_rows = repeat(question, other_question)
    got = lax.all_to_all(spread_rows, "ctx", 0, 0, axis_index_groups=Z_GROUPS)
    columns = [columns[0], *gate(columns[1:], got)]
    piece = pick(anchor_index, columns)
    below, above = along_z(piece, 1)
    send = question_pass(block_lengths, got, columns)
    parts = lax.all_to_all(send, "ctx", 0, 0, axis_index_groups=Z_GROUPS)
    distance = (lax.axis_index("ctx") // (NY * NC) - anchor_index[0] // (NY * NC)) & (NZ - 1)
    piece = jnp.where(distance == 1, below, jnp.where(distance == NZ - 1, above, piece))
    below, above = along_z(piece, 3)
    near = (distance < 2) | (distance == NZ - 1)
    piece = jnp.where(near, piece, jnp.where(distance < 5, below, above))
    spread = combine(question_length, parts, piece)
    own = lax.all_to_all(spread, "ctx", 0, 0, axis_index_groups=CHIP_GROUPS)
    pieces = [piece, lax.ppermute(piece, "ctx", Y_PARTNER)]
    pieces = pieces + [swap(piece), lax.ppermute(piece, "ctx", DIAGONAL)]
    mixed, key_cache, value_cache, token = encode(
        anchor_index,
        block_lengths,
        context_q,
        context_k,
        context_v,
        pieces,
    )
    (own,) = gate([own], token)
    answer = assemble(swap(own), assemble(own)).reshape(256, 2048)
    return mixed, key_cache, value_cache, answer


def solution(mesh):
    placed = (
        P("ctx", "heads"),
        P("ctx", "heads"),
        P("ctx", "heads"),
        P("ctx", "heads"),
        P(),
        P(),
        P(),
    )
    return jax.shard_map(
        on_device,
        mesh=mesh,
        in_specs=placed,
        out_specs=(P("ctx", "heads"), P("ctx", "heads"), P("ctx", "heads"), P(None, "heads")),
        check_vma=False,
    )
```

```python
import functools
import math

import jax
import jax.numpy as jnp
from jax import lax
from jax.experimental import pallas as pl
from jax.experimental.pallas import tpu as pltpu
from jax.sharding import PartitionSpec as P

HD = 128
SC = HD ** (-0.5)
SC2 = SC * math.log2(math.e)
NZ, NY, NC = 8, 4, 2
BLK = 256
BF = jnp.bfloat16
F32 = jnp.float32
SMEM = pl.BlockSpec(memory_space=pltpu.SMEM)
VMEM = pl.BlockSpec(memory_space=pltpu.VMEM)
SMALL = pltpu.CompilerParams(vmem_limit_bytes=4 * 1024 * 1024)
PARAMS = pltpu.CompilerParams(vmem_limit_bytes=20 * 1024 * 1024)


def index_of(z, y, c):
    return (z * NY + y) * NC + c


def permutation(move):
    return [
        (index_of(z, y, c), index_of(*move(z, y, c)))
        for z in range(NZ)
        for y in range(NY)
        for c in range(NC)
    ]


Z_ORDER = (0, 2, 4, 6, 1, 3, 5, 7)
Z_GROUPS = [[index_of(z, y, c) for z in Z_ORDER] for y in range(NY) for c in range(NC)]
CHIP_GROUPS = [[index_of(z, y, c) for y in range(NY) for z in Z_ORDER] for c in range(NC)]
OTHER_CORE = permutation(lambda z, y, c: (z, y, 1 - c))
Y_PARTNER = permutation(lambda z, y, c: (z, y ^ 1, c))
DIAGONAL = permutation(lambda z, y, c: (z, y ^ 1, 1 - c))
Y_MOVES = [permutation(lambda z, y, c, d=d: (z, y ^ d, c)) for d in range(NY)]
Z_SHIFTS = [permutation(lambda z, y, c, d=d: ((z + d) % NZ, y, c)) for d in range(NZ)]


def coordinates():
    place = lax.axis_index("ctx")
    return place // (NY * NC), (place // NC) % NY, place % NC


def sign_table():
    shape = (HD, HD)
    both = lax.broadcasted_iota(jnp.int32, shape, 0) & lax.broadcasted_iota(jnp.int32, shape, 1)
    both = both ^ (both >> 4)
    both = both ^ (both >> 2)
    both = both ^ (both >> 1)
    return (1 - 2 * (both & 1)).astype(F32).astype(BF)


def across(a, b):
    return lax.dot_general(a, b, (((1,), (1,)), ((), ())), preferred_element_type=F32)


def dot(a, b):
    return jnp.dot(a, b, preferred_element_type=F32)


def rotated(rows, table):
    return (dot(rows, table) * SC).astype(BF)


def join_kernel(mine_ref, k_ref, v_ref, early_ref, both_ref):
    c = coordinates()[2]
    both_ref[0 : 2 * BLK, :] = mine_ref[...]
    for head in range(NC):

        @pl.when(c == head)
        def _(head=head):
            lanes = slice(HD * head, HD * head + HD)
            both_ref[2 * BLK : 3 * BLK, :] = k_ref[:, lanes]
            both_ref[3 * BLK : 4 * BLK, :] = v_ref[:, lanes]


def join(mine, k_other, v_other, early):
    return pl.pallas_call(
        join_kernel,
        out_shape=jax.ShapeDtypeStruct((4 * BLK, HD), BF),
        in_specs=[VMEM] * 3 + [pl.BlockSpec(memory_space=pl.ANY)],
        out_specs=VMEM,
        compiler_params=SMALL,
        name="join",
    )(mine, k_other, v_other, early)


def repeat_kernel(own_ref, other_ref, send_ref, rows_ref):
    c = coordinates()[2]
    own, other = own_ref[...].astype(F32), other_ref[...].astype(F32)
    first, second = jnp.where(c == 0, own, other), jnp.where(c == 0, other, own)
    for at, source in enumerate((first, second)):
        for j in range(8):
            left, right = source[:, HD * j : HD * j + HD], source[:, HD * (8 + j) : HD * (9 + j)]
            rows_ref[8 * j + 4 * at : 8 * j + 4 * at + 4, :] = jnp.where(c == 0, left, right)
    rows = rows_ref[...].astype(BF)
    for i in range(NZ):
        send_ref[i] = rows


def repeat(own, other):
    return pl.pallas_call(
        repeat_kernel,
        out_shape=jax.ShapeDtypeStruct((NZ, 64, HD), BF),
        in_specs=[VMEM] * 2,
        out_specs=VMEM,
        scratch_shapes=[pltpu.VMEM((64, HD), F32)],
        compiler_params=SMALL,
        name="repeat",
    )(own, other)


def gate_kernel(*refs):
    pass


def gate(arrays, token):
    anywhere = pl.BlockSpec(memory_space=pl.ANY)
    return pl.pallas_call(
        gate_kernel,
        out_shape=[jax.ShapeDtypeStruct(x.shape, x.dtype) for x in arrays],
        in_specs=[anywhere] * (len(arrays) + 1),
        out_specs=[anywhere] * len(arrays),
        input_output_aliases={i: i for i in range(len(arrays))},
        compiler_params=pltpu.CompilerParams(vmem_limit_bytes=1024 * 1024),
        name="gate",
    )(*arrays, token)


def pick_kernel(anchor_ref, *refs):
    columns, out_ref = refs[:NY], refs[NY]
    z, y, c = coordinates()
    wanted = lax.rem(anchor_ref[0], NY * NC)
    rows = HD * lax.rem(y, 2)
    for which in range(8):
        core = c if which < NY else 1 - c
        place = NC * (y ^ which % NY) + core

        @pl.when(place == wanted)
        def _(which=which):
            for i in range(2):
                first = pl.multiple_of(2 * BLK * (which // NY) + BLK * i + rows, HD)
                out_ref[HD * i : HD * i + HD, :] = columns[which % NY][pl.ds(first, HD), :]


def pick(anchor_index, columns):
    return pl.pallas_call(
        pick_kernel,
        out_shape=jax.ShapeDtypeStruct((BLK, HD), BF),
        in_specs=[SMEM] + [VMEM] * NY,
        out_specs=VMEM,
        compiler_params=SMALL,
        name="pick",
    )(anchor_index, *columns)


def thirds(x):
    high = x.astype(BF)
    rest = x - high.astype(F32)
    middle = rest.astype(BF)
    return high, middle, (rest - middle.astype(F32)).astype(BF)


def question_kernel(lengths_ref, got_ref, *refs):
    columns, send_ref = refs[:NY], refs[NY]
    z, y, c = coordinates()
    table = sign_table()
    lane = lax.broadcasted_iota(jnp.int32, (BLK, BLK), 1)
    ids = [index_of(z, y ^ d, c) for d in range(NY)]
    ids += [index_of(z, y ^ d, 1 - c) for d in range(NY)]
    q = rotated(got_ref[...].reshape(NZ * 64, HD), table)
    turned = [rotated(column[...], table) for column in columns]
    tops, totals, sums = [], [], []
    for i in range(2):
        chunk = q[BLK * i : BLK * i + BLK]
        top = total = summed = None
        for which in range(8):
            column, first = turned[which % NY], 2 * BLK * (which // NY)
            k, v = column[first : first + BLK], column[first + BLK : first + 2 * BLK]
            part = jnp.where(lane < lengths_ref[ids[which]], across(chunk, k) * SC2, -jnp.inf)
            m = jnp.max(part, axis=1, keepdims=True)
            e = jnp.exp2(part - m)
            d = jnp.sum(e, axis=1, keepdims=True)
            n = dot(e.astype(BF), v)
            if which == 0:
                top, total, summed = m, d, n
            else:
                new = jnp.maximum(top, m)
                old_scale, scale = jnp.exp2(top - new), jnp.exp2(m - new)
                top = new
                total = total * old_scale + d * scale
                summed = summed * old_scale + n * scale
        tops.append(top)
        totals.append(total)
        sums.append(summed)
    lanes = lax.broadcasted_iota(jnp.int32, (HD, HD), 1)
    packed = jnp.zeros((HD, HD), F32)
    for i in range(4):
        rows = slice(HD * (i % 2), HD * (i % 2) + HD)
        packed = jnp.where(lanes == i, tops[i // 2][rows], packed)
        packed = jnp.where(lanes == 4 + i, totals[i // 2][rows], packed)
    tile = packed.T[0:8, :]
    for i in range(2):
        send_ref[4 * i : 4 * i + 4, 0:64, :] = sums[i].reshape(4, 64, HD)
    for i in range(NZ):
        send_ref[i, 64:72, :] = tile


def question_pass(lengths, got, columns):
    return pl.pallas_call(
        question_kernel,
        out_shape=jax.ShapeDtypeStruct((NZ, 72, HD), F32),
        in_specs=[SMEM] + [VMEM] * (1 + NY),
        out_specs=VMEM,
        compiler_params=PARAMS,
        cost_estimate=pl.CostEstimate(
            flops=900_000_000, bytes_accessed=2_500_000, transcendentals=1_100_000
        ),
        name="question_pass",
    )(lengths, got, *columns)


def combine_kernel(limit_ref, parts_ref, piece_ref, early_ref, send_ref, columns_ref):
    z, y, c = coordinates()
    table = sign_table()
    rank = z % 2 * 4 + z // 2
    tops = [parts_ref[s, pl.ds(64 + rank // 2, 1), :] for s in range(NZ)]
    totals = [parts_ref[s, pl.ds(68 + rank // 2, 1), :] for s in range(NZ)]
    tops, totals = jnp.concatenate(tops, axis=0), jnp.concatenate(totals, axis=0)
    weights = jnp.exp2(tops - jnp.max(tops, axis=0, keepdims=True))
    weights = weights / jnp.sum(weights * totals, axis=0, keepdims=True)
    square = jnp.concatenate([weights, jnp.zeros((HD - NZ, HD), F32)], axis=0)
    columns_ref[...] = square.T
    columns = columns_ref[pl.ds(pl.multiple_of(rank % 2 * 64, 64), 64), :]
    row = lax.broadcasted_iota(jnp.int32, (64, HD), 0)
    result = jnp.zeros((64, HD), F32)
    for s in range(NZ):
        result = result + columns[:, s : s + 1] * parts_ref[s, 0:64, :]
    high, middle, low = thirds(result)
    back = (dot(low, table) + dot(middle, table) + dot(high, table)) * SC
    position = (z * NY + y) * 8 + (row & 7)
    back = jnp.where(position < limit_ref[0], back, 0.0)
    back = jnp.concatenate([back[8 * j : 8 * j + 8] for j in range(8)], axis=1).astype(BF)
    for i in range(NZ * NY):
        send_ref[i] = back


def combine(limit, parts, piece, early):
    return pl.pallas_call(
        combine_kernel,
        out_shape=jax.ShapeDtypeStruct((NZ * NY, 8, 1024), BF),
        in_specs=[SMEM, VMEM] + [pl.BlockSpec(memory_space=pl.ANY)] * 2,
        out_specs=VMEM,
        scratch_shapes=[pltpu.VMEM((HD, HD), F32)],
        compiler_params=SMALL,
        name="combine",
    )(limit, parts, piece, early)


def caches_kernel(k_ref, v_ref, krot_ref, vrot_ref):
    table = sign_table()
    for g in range(2):
        lanes = slice(HD * g, HD * g + HD)
        krot_ref[:, lanes] = rotated(k_ref[:, lanes], table)
        vrot_ref[:, lanes] = rotated(v_ref[:, lanes], table)


def caches(k, v):
    return pl.pallas_call(
        caches_kernel,
        out_shape=(jax.ShapeDtypeStruct(k.shape, BF), jax.ShapeDtypeStruct(v.shape, BF)),
        in_specs=[VMEM] * 2,
        out_specs=(VMEM, VMEM),
        compiler_params=SMALL,
        name="caches",
    )(k, v)


def encode_kernel(anchor_ref, lengths_ref, q_ref, k_ref, v_ref, *refs):
    pieces = refs[:4]
    mixed_ref, token_ref, far_k_ref, far_v_ref = refs[4:]
    z, y, c = coordinates()
    place = index_of(z, y, c)
    anchor = anchor_ref[0]
    k, v = k_ref[...], v_ref[...]
    token_ref[...] = jnp.zeros_like(token_ref)
    g = pl.program_id(0)
    for core in range(2):

        @pl.when((g == c) == (core == 0))
        def _(core=core):
            for i in range(2):
                at = pl.multiple_of(HD * lax.rem(y + i, 2), HD)
                far_k_ref[pl.ds(at, HD), :] = pieces[2 * core + i][0:HD, :]
                far_v_ref[pl.ds(at, HD), :] = pieces[2 * core + i][HD : 2 * HD, :]

    far_k, far_v = far_k_ref[...], far_v_ref[...]
    far_len = jnp.where(place == anchor, 0, lengths_ref[anchor])
    own_len = lengths_ref[place]
    query = lax.broadcasted_iota(jnp.int32, (BLK, BLK), 0)
    key = lax.broadcasted_iota(jnp.int32, (BLK, BLK), 1)
    far_ok = key < far_len
    own_ok = (key <= query) & (key < own_len)
    for j in range(8):
        q = q_ref[:, HD * j : HD * j + HD]
        s_far = jnp.where(far_ok, across(q, far_k) * SC2, -jnp.inf)
        s_own = jnp.where(own_ok, across(q, k) * SC2, -jnp.inf)
        top = jnp.max(jnp.maximum(s_far, s_own), axis=1, keepdims=True)
        e_far = jnp.exp2(s_far - top)
        e_own = jnp.exp2(s_own - top)
        total = jnp.sum(e_far + e_own, axis=1, keepdims=True)
        summed = dot(e_far.astype(BF), far_v) + dot(e_own.astype(BF), v)
        mixed_ref[:, HD * j : HD * j + HD] = (summed / total).astype(BF)


def encode(anchor_index, lengths, q, k, v, pieces):
    heads = pl.BlockSpec((BLK, 8 * HD), lambda g: (0, g))
    group = pl.BlockSpec((BLK, HD), lambda g: (0, g))
    token = pl.BlockSpec((8, HD), lambda g: (0, 0))
    return pl.pallas_call(
        encode_kernel,
        grid=(2,),
        out_shape=(
            jax.ShapeDtypeStruct(q.shape, BF),
            jax.ShapeDtypeStruct((8, HD), F32),
        ),
        in_specs=[SMEM, SMEM, heads, group, group] + [VMEM] * 4,
        out_specs=(heads, token),
        scratch_shapes=[pltpu.VMEM((BLK, HD), BF), pltpu.VMEM((BLK, HD), BF)],
        compiler_params=PARAMS,
        cost_estimate=pl.CostEstimate(
            flops=1_100_000_000, bytes_accessed=3_500_000, transcendentals=2_100_000
        ),
        name="encode",
    )(anchor_index, lengths, q, k, v, *pieces)


def assemble_kernel(part_ref, *refs, own):
    out_ref, sems = refs[-2:]
    c = coordinates()[2]
    lanes = pl.ds(pl.multiple_of(1024 * (c if own else 1 - c), 1024), 1024)
    copies = []
    for y in range(NY):
        for odd in range(2):
            source = part_ref.at[pl.ds(NZ * y + 4 * odd, 4)]
            target = out_ref.at[:, odd, y, :, lanes]
            copies.append(pltpu.make_async_copy(source, target, sems.at[y, odd]))
    for copy in copies:
        copy.start()
    for copy in copies:
        copy.wait()


def assemble(part, out=None):
    anywhere = pl.BlockSpec(memory_space=pl.ANY)
    return pl.pallas_call(
        functools.partial(assemble_kernel, own=out is None),
        out_shape=jax.ShapeDtypeStruct((NZ // 2, 2, NY, 8, 2048), BF),
        in_specs=[anywhere] * (1 if out is None else 2),
        out_specs=anywhere,
        scratch_shapes=[pltpu.SemaphoreType.DMA((NY, 2))],
        input_output_aliases={} if out is None else {1: 0},
        compiler_params=SMALL,
        name="assemble",
    )(part, *([] if out is None else [out]))


def on_device(
    context_q, context_k, context_v, question, block_lengths, anchor_index, question_length
):
    def swap(x):
        return lax.ppermute(x, "ctx", OTHER_CORE)

    def along_y(x):
        return [x] + [lax.ppermute(x, "ctx", Y_MOVES[d]) for d in range(1, NY)]

    def along_z(x, d):
        return lax.ppermute(x, "ctx", Z_SHIFTS[d]), lax.ppermute(x, "ctx", Z_SHIFTS[NZ - d])

    def with_other_core(parts):
        return parts + [swap(x) for x in parts]

    first_lane = lax.axis_index("ctx") % NC * HD
    halves = [lax.dynamic_slice_in_dim(x, first_lane, HD, 1) for x in (context_k, context_v)]
    mine = jnp.concatenate(halves, axis=0)
    other_question = swap(question)
    columns = along_y(join(mine, swap(context_k), swap(context_v), other_question))
    spread_rows = repeat(question, other_question)
    got = lax.all_to_all(spread_rows, "ctx", 0, 0, axis_index_groups=Z_GROUPS)
    columns = [columns[0], *gate(columns[1:], got)]
    piece = pick(anchor_index, columns)
    below, above = along_z(piece, 1)
    send = question_pass(block_lengths, got, columns)
    parts = lax.all_to_all(send, "ctx", 0, 0, axis_index_groups=Z_GROUPS)
    distance = (lax.axis_index("ctx") // (NY * NC) - anchor_index[0] // (NY * NC)) & (NZ - 1)
    piece = jnp.where(distance == 1, below, jnp.where(distance == NZ - 1, above, piece))
    below, above = along_z(piece, 3)
    near = (distance < 2) | (distance == NZ - 1)
    piece = jnp.where(near, piece, jnp.where(distance < 5, below, above))
    key_cache, value_cache = caches(context_k, context_v)
    spread = combine(question_length, parts, piece, value_cache)
    own = lax.all_to_all(spread, "ctx", 0, 0, axis_index_groups=CHIP_GROUPS)
    pieces = [piece, lax.ppermute(piece, "ctx", Y_PARTNER)]
    pieces = pieces + [swap(piece), lax.ppermute(piece, "ctx", DIAGONAL)]
    mixed, token = encode(
        anchor_index,
        block_lengths,
        context_q,
        context_k,
        context_v,
        pieces,
    )
    (own,) = gate([own], token)
    answer = assemble(swap(own), assemble(own)).reshape(256, 2048)
    return mixed, key_cache, value_cache, answer


def solution(mesh):
    placed = (
        P("ctx", "heads"),
        P("ctx", "heads"),
        P("ctx", "heads"),
        P("ctx", "heads"),
        P(),
        P(),
        P(),
    )
    return jax.shard_map(
        on_device,
        mesh=mesh,
        in_specs=placed,
        out_specs=(P("ctx", "heads"), P("ctx", "heads"), P("ctx", "heads"), P(None, "heads")),
        check_vma=False,
    )
```

```python
import functools
import math

import jax
import jax.numpy as jnp
from jax import lax
from jax.experimental import pallas as pl
from jax.experimental.pallas import tpu as pltpu
from jax.sharding import PartitionSpec as P

HD = 128
SC = HD ** (-0.5)
SC2 = SC * math.log2(math.e)
NZ, NY, NC = 8, 4, 2
BLK = 256
BF = jnp.bfloat16
F32 = jnp.float32
SMEM = pl.BlockSpec(memory_space=pltpu.SMEM)
VMEM = pl.BlockSpec(memory_space=pltpu.VMEM)
SMALL = pltpu.CompilerParams(vmem_limit_bytes=4 * 1024 * 1024)
PARAMS = pltpu.CompilerParams(vmem_limit_bytes=20 * 1024 * 1024)


def index_of(z, y, c):
    return (z * NY + y) * NC + c


def permutation(move):
    return [
        (index_of(z, y, c), index_of(*move(z, y, c)))
        for z in range(NZ)
        for y in range(NY)
        for c in range(NC)
    ]


Z_ORDER = (0, 2, 4, 6, 1, 3, 5, 7)
Z_GROUPS = [[index_of(z, y, c) for z in Z_ORDER] for y in range(NY) for c in range(NC)]
CHIP_GROUPS = [[index_of(z, y, c) for y in range(NY) for z in Z_ORDER] for c in range(NC)]
OTHER_CORE = permutation(lambda z, y, c: (z, y, 1 - c))
Y_PARTNER = permutation(lambda z, y, c: (z, y ^ 1, c))
Y_MOVES = [permutation(lambda z, y, c, d=d: (z, y ^ d, c)) for d in range(NY)]
Z_SHIFTS = [permutation(lambda z, y, c, d=d: ((z + d) % NZ, y, c)) for d in range(NZ)]


def coordinates():
    place = lax.axis_index("ctx")
    return place // (NY * NC), (place // NC) % NY, place % NC


def sign_table():
    shape = (HD, HD)
    both = lax.broadcasted_iota(jnp.int32, shape, 0) & lax.broadcasted_iota(jnp.int32, shape, 1)
    both = both ^ (both >> 4)
    both = both ^ (both >> 2)
    both = both ^ (both >> 1)
    return (1 - 2 * (both & 1)).astype(F32).astype(BF)


def across(a, b):
    return lax.dot_general(a, b, (((1,), (1,)), ((), ())), preferred_element_type=F32)


def dot(a, b):
    return jnp.dot(a, b, preferred_element_type=F32)


def rotated(rows, table):
    return (dot(rows, table) * SC).astype(BF)


def join_kernel(mine_ref, k_ref, v_ref, early_ref, both_ref):
    c = coordinates()[2]
    both_ref[0 : 2 * BLK, :] = mine_ref[...]
    for head in range(NC):

        @pl.when(c == head)
        def _(head=head):
            lanes = slice(HD * head, HD * head + HD)
            both_ref[2 * BLK : 3 * BLK, :] = k_ref[:, lanes]
            both_ref[3 * BLK : 4 * BLK, :] = v_ref[:, lanes]


def join(mine, k_other, v_other, early):
    return pl.pallas_call(
        join_kernel,
        out_shape=jax.ShapeDtypeStruct((4 * BLK, HD), BF),
        in_specs=[VMEM] * 3 + [pl.BlockSpec(memory_space=pl.ANY)],
        out_specs=VMEM,
        compiler_params=SMALL,
        name="join",
    )(mine, k_other, v_other, early)


def repeat_kernel(own_ref, other_ref, send_ref, rows_ref):
    c = coordinates()[2]
    own, other = own_ref[...].astype(F32), other_ref[...].astype(F32)
    first, second = jnp.where(c == 0, own, other), jnp.where(c == 0, other, own)
    for at, source in enumerate((first, second)):
        for j in range(8):
            left, right = source[:, HD * j : HD * j + HD], source[:, HD * (8 + j) : HD * (9 + j)]
            rows_ref[8 * j + 4 * at : 8 * j + 4 * at + 4, :] = jnp.where(c == 0, left, right)
    rows = rows_ref[...].astype(BF)
    for i in range(NZ):
        send_ref[i] = rows


def repeat(own, other):
    return pl.pallas_call(
        repeat_kernel,
        out_shape=jax.ShapeDtypeStruct((NZ, 64, HD), BF),
        in_specs=[VMEM] * 2,
        out_specs=VMEM,
        scratch_shapes=[pltpu.VMEM((64, HD), F32)],
        compiler_params=SMALL,
        name="repeat",
    )(own, other)


def gate_kernel(*refs):
    pass


def gate(arrays, token):
    anywhere = pl.BlockSpec(memory_space=pl.ANY)
    return pl.pallas_call(
        gate_kernel,
        out_shape=[jax.ShapeDtypeStruct(x.shape, x.dtype) for x in arrays],
        in_specs=[anywhere] * (len(arrays) + 1),
        out_specs=[anywhere] * len(arrays),
        input_output_aliases={i: i for i in range(len(arrays))},
        compiler_params=pltpu.CompilerParams(vmem_limit_bytes=1024 * 1024),
        name="gate",
    )(*arrays, token)


def pick_kernel(anchor_ref, *refs):
    columns, out_ref = refs[:NY], refs[NY]
    z, y, c = coordinates()
    wanted = lax.rem(anchor_ref[0], NY * NC)
    rows = HD * lax.rem(y, 2)
    for which in range(8):
        core = c if which < NY else 1 - c
        place = NC * (y ^ which % NY) + core

        @pl.when(place == wanted)
        def _(which=which):
            for i in range(2):
                first = pl.multiple_of(2 * BLK * (which // NY) + BLK * i + rows, HD)
                out_ref[HD * i : HD * i + HD, :] = columns[which % NY][pl.ds(first, HD), :]


def pick(anchor_index, columns):
    return pl.pallas_call(
        pick_kernel,
        out_shape=jax.ShapeDtypeStruct((BLK, HD), BF),
        in_specs=[SMEM] + [VMEM] * NY,
        out_specs=VMEM,
        compiler_params=SMALL,
        name="pick",
    )(anchor_index, *columns)


def thirds(x):
    high = x.astype(BF)
    rest = x - high.astype(F32)
    middle = rest.astype(BF)
    return high, middle, (rest - middle.astype(F32)).astype(BF)


def question_kernel(lengths_ref, got_ref, *refs):
    columns, send_ref = refs[:NY], refs[NY]
    z, y, c = coordinates()
    table = sign_table()
    lane = lax.broadcasted_iota(jnp.int32, (BLK, BLK), 1)
    ids = [index_of(z, y ^ d, c) for d in range(NY)]
    ids += [index_of(z, y ^ d, 1 - c) for d in range(NY)]
    q = rotated(got_ref[...].reshape(NZ * 64, HD), table)
    turned = [rotated(column[...], table) for column in columns]
    tops, totals, sums = [], [], []
    for i in range(2):
        chunk = q[BLK * i : BLK * i + BLK]
        top = total = summed = None
        for which in range(8):
            column, first = turned[which % NY], 2 * BLK * (which // NY)
            k, v = column[first : first + BLK], column[first + BLK : first + 2 * BLK]
            part = jnp.where(lane < lengths_ref[ids[which]], across(chunk, k) * SC2, -jnp.inf)
            m = jnp.max(part, axis=1, keepdims=True)
            e = jnp.exp2(part - m)
            d = jnp.sum(e, axis=1, keepdims=True)
            n = dot(e.astype(BF), v)
            if which == 0:
                top, total, summed = m, d, n
            else:
                new = jnp.maximum(top, m)
                old_scale, scale = jnp.exp2(top - new), jnp.exp2(m - new)
                top = new
                total = total * old_scale + d * scale
                summed = summed * old_scale + n * scale
        tops.append(top)
        totals.append(total)
        sums.append(summed)
    lanes = lax.broadcasted_iota(jnp.int32, (HD, HD), 1)
    packed = jnp.zeros((HD, HD), F32)
    for i in range(4):
        rows = slice(HD * (i % 2), HD * (i % 2) + HD)
        packed = jnp.where(lanes == i, tops[i // 2][rows], packed)
        packed = jnp.where(lanes == 4 + i, totals[i // 2][rows], packed)
    tile = packed.T[0:8, :]
    for i in range(2):
        send_ref[4 * i : 4 * i + 4, 0:64, :] = sums[i].reshape(4, 64, HD)
    for i in range(NZ):
        send_ref[i, 64:72, :] = tile


def question_pass(lengths, got, columns):
    return pl.pallas_call(
        question_kernel,
        out_shape=jax.ShapeDtypeStruct((NZ, 72, HD), F32),
        in_specs=[SMEM] + [VMEM] * (1 + NY),
        out_specs=VMEM,
        compiler_params=PARAMS,
        cost_estimate=pl.CostEstimate(
            flops=900_000_000, bytes_accessed=2_500_000, transcendentals=1_100_000
        ),
        name="question_pass",
    )(lengths, got, *columns)


def combine_kernel(limit_ref, parts_ref, piece_ref, early_ref, send_ref, columns_ref):
    z, y, c = coordinates()
    table = sign_table()
    rank = z % 2 * 4 + z // 2
    tops = [parts_ref[s, pl.ds(64 + rank // 2, 1), :] for s in range(NZ)]
    totals = [parts_ref[s, pl.ds(68 + rank // 2, 1), :] for s in range(NZ)]
    tops, totals = jnp.concatenate(tops, axis=0), jnp.concatenate(totals, axis=0)
    weights = jnp.exp2(tops - jnp.max(tops, axis=0, keepdims=True))
    weights = weights / jnp.sum(weights * totals, axis=0, keepdims=True)
    square = jnp.concatenate([weights, jnp.zeros((HD - NZ, HD), F32)], axis=0)
    columns_ref[...] = square.T
    columns = columns_ref[pl.ds(pl.multiple_of(rank % 2 * 64, 64), 64), :]
    row = lax.broadcasted_iota(jnp.int32, (64, HD), 0)
    result = jnp.zeros((64, HD), F32)
    for s in range(NZ):
        result = result + columns[:, s : s + 1] * parts_ref[s, 0:64, :]
    high, middle, low = thirds(result)
    back = (dot(low, table) + dot(middle, table) + dot(high, table)) * SC
    position = (z * NY + y) * 8 + (row & 7)
    back = jnp.where(position < limit_ref[0], back, 0.0)
    back = jnp.concatenate([back[8 * j : 8 * j + 8] for j in range(8)], axis=1).astype(BF)
    for i in range(NZ * NY):
        send_ref[i] = back


def combine(limit, parts, piece, early):
    return pl.pallas_call(
        combine_kernel,
        out_shape=jax.ShapeDtypeStruct((NZ * NY, 8, 1024), BF),
        in_specs=[SMEM, VMEM] + [pl.BlockSpec(memory_space=pl.ANY)] * 2,
        out_specs=VMEM,
        scratch_shapes=[pltpu.VMEM((HD, HD), F32)],
        compiler_params=SMALL,
        name="combine",
    )(limit, parts, piece, early)


def caches_kernel(k_ref, v_ref, krot_ref, vrot_ref):
    table = sign_table()
    for g in range(2):
        lanes = slice(HD * g, HD * g + HD)
        krot_ref[:, lanes] = rotated(k_ref[:, lanes], table)
        vrot_ref[:, lanes] = rotated(v_ref[:, lanes], table)


def caches(k, v):
    return pl.pallas_call(
        caches_kernel,
        out_shape=(jax.ShapeDtypeStruct(k.shape, BF), jax.ShapeDtypeStruct(v.shape, BF)),
        in_specs=[VMEM] * 2,
        out_specs=(VMEM, VMEM),
        compiler_params=SMALL,
        name="caches",
    )(k, v)


def encode_kernel(anchor_ref, lengths_ref, q_ref, k_ref, v_ref, *refs):
    pieces = refs[:4]
    mixed_ref, token_ref, far_k_ref, far_v_ref = refs[4:]
    z, y, c = coordinates()
    place = index_of(z, y, c)
    anchor = anchor_ref[0]
    k, v = k_ref[...], v_ref[...]
    token_ref[...] = jnp.zeros_like(token_ref)
    g = pl.program_id(0)
    for core in range(2):

        @pl.when((g == c) == (core == 0))
        def _(core=core):
            for i in range(2):
                at = pl.multiple_of(HD * lax.rem(y + i, 2), HD)
                far_k_ref[pl.ds(at, HD), :] = pieces[2 * core + i][0:HD, :]
                far_v_ref[pl.ds(at, HD), :] = pieces[2 * core + i][HD : 2 * HD, :]

    far_k, far_v = far_k_ref[...], far_v_ref[...]
    far_len = jnp.where(place == anchor, 0, lengths_ref[anchor])
    own_len = lengths_ref[place]
    query = lax.broadcasted_iota(jnp.int32, (BLK, BLK), 0)
    key = lax.broadcasted_iota(jnp.int32, (BLK, BLK), 1)
    far_ok = key < far_len
    own_ok = (key <= query) & (key < own_len)
    for j in range(8):
        q = q_ref[:, HD * j : HD * j + HD]
        s_far = jnp.where(far_ok, across(q, far_k) * SC2, -jnp.inf)
        s_own = jnp.where(own_ok, across(q, k) * SC2, -jnp.inf)
        top = jnp.max(jnp.maximum(s_far, s_own), axis=1, keepdims=True)
        e_far = jnp.exp2(s_far - top)
        e_own = jnp.exp2(s_own - top)
        total = jnp.sum(e_far + e_own, axis=1, keepdims=True)
        summed = dot(e_far.astype(BF), far_v) + dot(e_own.astype(BF), v)
        mixed_ref[:, HD * j : HD * j + HD] = (summed / total).astype(BF)


def encode(anchor_index, lengths, q, k, v, pieces):
    heads = pl.BlockSpec((BLK, 8 * HD), lambda g: (0, g))
    group = pl.BlockSpec((BLK, HD), lambda g: (0, g))
    token = pl.BlockSpec((8, HD), lambda g: (0, 0))
    return pl.pallas_call(
        encode_kernel,
        grid=(2,),
        out_shape=(
            jax.ShapeDtypeStruct(q.shape, BF),
            jax.ShapeDtypeStruct((8, HD), F32),
        ),
        in_specs=[SMEM, SMEM, heads, group, group] + [VMEM] * 4,
        out_specs=(heads, token),
        scratch_shapes=[pltpu.VMEM((BLK, HD), BF), pltpu.VMEM((BLK, HD), BF)],
        compiler_params=PARAMS,
        cost_estimate=pl.CostEstimate(
            flops=1_100_000_000, bytes_accessed=3_500_000, transcendentals=2_100_000
        ),
        name="encode",
    )(anchor_index, lengths, q, k, v, *pieces)


def assemble_kernel(part_ref, *refs, own):
    out_ref, sems = refs[-2:]
    c = coordinates()[2]
    lanes = pl.ds(pl.multiple_of(1024 * (c if own else 1 - c), 1024), 1024)
    copies = []
    for y in range(NY):
        for odd in range(2):
            source = part_ref.at[pl.ds(NZ * y + 4 * odd, 4)]
            target = out_ref.at[:, odd, y, :, lanes]
            copies.append(pltpu.make_async_copy(source, target, sems.at[y, odd]))
    for copy in copies:
        copy.start()
    for copy in copies:
        copy.wait()


def assemble(part, out=None):
    anywhere = pl.BlockSpec(memory_space=pl.ANY)
    return pl.pallas_call(
        functools.partial(assemble_kernel, own=out is None),
        out_shape=jax.ShapeDtypeStruct((NZ // 2, 2, NY, 8, 2048), BF),
        in_specs=[anywhere] * (1 if out is None else 2),
        out_specs=anywhere,
        scratch_shapes=[pltpu.SemaphoreType.DMA((NY, 2))],
        input_output_aliases={} if out is None else {1: 0},
        compiler_params=SMALL,
        name="assemble",
    )(part, *([] if out is None else [out]))


def on_device(
    context_q, context_k, context_v, question, block_lengths, anchor_index, question_length
):
    def swap(x):
        return lax.ppermute(x, "ctx", OTHER_CORE)

    def along_y(x):
        return [x] + [lax.ppermute(x, "ctx", Y_MOVES[d]) for d in range(1, NY)]

    def along_z(x, d):
        return lax.ppermute(x, "ctx", Z_SHIFTS[d]), lax.ppermute(x, "ctx", Z_SHIFTS[NZ - d])

    def with_other_core(parts):
        return parts + [swap(x) for x in parts]

    first_lane = lax.axis_index("ctx") % NC * HD
    halves = [lax.dynamic_slice_in_dim(x, first_lane, HD, 1) for x in (context_k, context_v)]
    mine = jnp.concatenate(halves, axis=0)
    other_question = swap(question)
    columns = along_y(join(mine, swap(context_k), swap(context_v), other_question))
    spread_rows = repeat(question, other_question)
    got = lax.all_to_all(spread_rows, "ctx", 0, 0, axis_index_groups=Z_GROUPS)
    columns = [columns[0], *gate(columns[1:], got)]
    piece = pick(anchor_index, columns)
    below, above = along_z(piece, 1)
    send = question_pass(block_lengths, got, columns)
    parts = lax.all_to_all(send, "ctx", 0, 0, axis_index_groups=Z_GROUPS)
    distance = (lax.axis_index("ctx") // (NY * NC) - anchor_index[0] // (NY * NC)) & (NZ - 1)
    piece = jnp.where(distance == 1, below, jnp.where(distance == NZ - 1, above, piece))
    below, above = along_z(piece, 3)
    near = (distance < 2) | (distance == NZ - 1)
    piece = jnp.where(near, piece, jnp.where(distance < 5, below, above))
    key_cache, value_cache = caches(context_k, context_v)
    spread = combine(question_length, parts, piece, value_cache)
    own = lax.all_to_all(spread, "ctx", 0, 0, axis_index_groups=CHIP_GROUPS)
    pieces = [piece, lax.ppermute(piece, "ctx", Y_PARTNER)]
    pieces = pieces + [swap(x) for x in pieces]
    mixed, token = encode(
        anchor_index,
        block_lengths,
        context_q,
        context_k,
        context_v,
        pieces,
    )
    (own,) = gate([own], token)
    answer = assemble(swap(own), assemble(own)).reshape(256, 2048)
    return mixed, key_cache, value_cache, answer


def solution(mesh):
    placed = (
        P("ctx", "heads"),
        P("ctx", "heads"),
        P("ctx", "heads"),
        P("ctx", "heads"),
        P(),
        P(),
        P(),
    )
    return jax.shard_map(
        on_device,
        mesh=mesh,
        in_specs=placed,
        out_specs=(P("ctx", "heads"), P("ctx", "heads"), P("ctx", "heads"), P(None, "heads")),
        check_vma=False,
    )
```
